256 devices in a mesh: row: 32 (over z, y_hi, core), col: 8 (over y_lo, x).
Axes of the slice: x: 4, y: 4 (y_hi: 2, y_lo: 2; y = y_hi * 2 + y_lo), z: 8, core: 2. Of those that a mesh axis runs over, the one named last changes fastest.
Arguments:
- queries: bfloat16 [32768, 512], P(('row', 'col')), may hold values from -6 to 6
- keys: bfloat16 [32768, 128], P(('row', 'col')), may hold values from -6 to 6
- values: bfloat16 [32768, 128], P(('row', 'col')), may hold values from -6 to 6
- outputs: bfloat16 [32768, 512], P(('row', 'col')), may hold values from -6 to 6
- out_grad: bfloat16 [32768, 512], P(('row', 'col')), may hold values from -4 to 4
- log_sum_exp: float32 [32768, 4], P(('row', 'col')), may hold values from 2 to 4
- segment_ids: int32 [32768], P(('row', 'col')), may hold values from 0 to 67, never falling along the last dimension, each value on 1 to 17408 neighbouring positions
Outputs:
- grad_queries: bfloat16 [32768, 512], P(('row', 'col'))
- grad_keys: bfloat16 [32768, 128], P(('row', 'col'))
- grad_values: bfloat16 [32768, 128], P(('row', 'col'))
The draws below stay inside these ranges and needn't reach their ends.
Inputs may be any that keep to these rules, and one draw needn't show every extreme that they name: `segment_ids`: segment numbers never fall along the tokens; each document holds at most 17408 tokens, and one holds exactly that many.
All inputs are finite; a program needn't handle non-finite values.
Results may differ from the reference program's by a relative error of at most 0.0053.
Values may be sent and summed in bfloat16 or wider, within the bound.
A program may use at most 64 MiB of HBM per device.

```python
import math
import jax
import jax.numpy as jnp
import numpy as np
from jax import lax

HD = 128
KVH = 1
GROUP = 4
TOK_DEV = 128
HQ = 4
TOKENS = 32768
N_COL = 8


def levels(key, extent, split, low, largest):
    level, own = 1.0, jax.random.fold_in(key, 6)
    for dim, blocks in split:
        draws = jnp.exp(jax.random.uniform(jax.random.fold_in(own, dim), (blocks,), jnp.float32, low / len(split), largest / len(split)))
        level = level * jnp.repeat(draws, extent[dim] // blocks).reshape([-1 if axis == dim else 1 for axis in range(len(extent))])
    return level


def profile(number_of, total, bound, skew):
    portions = [(1 << 20) // math.isqrt(standing ** skew) + 1 for standing in range(2, number_of + 1)]
    surplus, given = total - bound - (number_of - 1), [1] * (number_of - 1)
    while surplus > 0:
        movable = [i for i in range(number_of - 1) if given[i] < bound]
        whole, remaining = sum([portions[i] for i in movable]), surplus
        for i in movable:
            more = min(bound - given[i], max(1, remaining * portions[i] // whole), surplus)
            given[i] = given[i] + more
            surplus = surplus - more
    return np.array([bound] + given)


def uneven_parts(key, count, total, reach, lean):
    if count == 2:
        one = jax.random.randint(key, (), max(1, total - reach), min(reach, total - 1) + 1)
        return jnp.stack([one, total - one])
    sizes = jnp.asarray(profile(count, total, reach, lean), jnp.int32)
    twos = (count - 1) // 2
    source_of, receiver = sizes[1:1 + 2 * twos:2], sizes[2:2 + 2 * twos:2]
    slack = jnp.minimum(source_of - 1, reach - receiver)
    moved = jax.random.randint(jax.random.fold_in(key, 1), (twos,), 0, 1 << 20) % (slack + 1)
    sizes = sizes.at[1:1 + 2 * twos:2].set(source_of - moved).at[2:2 + 2 * twos:2].set(receiver + moved)
    return sizes[jax.random.permutation(jax.random.fold_in(key, 2), count)]


def noise(stream_key, shape, spread, bound, split=(), kind=jnp.bfloat16):
    result = spread * jax.random.normal(stream_key, shape, jnp.float32)
    if split:
        result = result * levels(stream_key, shape, split, -0.22, 0.18)
    return jnp.clip(result, -bound, bound).astype(kind)


def setup_inputs(seed: int = 0) -> dict:
    key_list = jax.random.split(jax.random.key(seed), 8)
    queries = noise(key_list[0], (TOKENS, HQ * HD), 1.0, 6.0, ((0, 256),))
    keys = noise(key_list[1], (TOKENS, KVH * HD), 1.0, 6.0, ((0, 256),))
    values = noise(key_list[2], (TOKENS, KVH * HD), 1.0, 6.0, ((0, 256),))
    outputs = noise(key_list[3], (TOKENS, HQ * HD), 1.0, 6.0, ((0, 256),))
    out_grad = noise(key_list[4], (TOKENS, HQ * HD), 0.25, 4.0, ((0, 256),))
    log_sum_exp = jnp.clip(2.0 + 2.0 * jax.random.uniform(key_list[5], (TOKENS, HQ), jnp.float32) ** levels(key_list[5], (TOKENS, HQ), ((0, 256),), -0.2, 0.2), 2.0, 4.0)
    segment_ids = jnp.searchsorted(jnp.cumsum(uneven_parts(key_list[6], TOKENS // 512 + 4, TOKENS, TOKENS // 2 + N_COL * TOK_DEV, 2)), jnp.arange(TOKENS), side="right").astype(jnp.int32)
    return {"queries": queries, "keys": keys, "values": values, "outputs": outputs, "out_grad": out_grad, "log_sum_exp": log_sum_exp, "segment_ids": segment_ids}


def reference(queries, keys, values, outputs, out_grad, log_sum_exp, segment_ids):
    scaling = HD ** -0.5
    head_count = KVH * GROUP
    block_rows = 512
    block_count = TOKENS // block_rows
    query_all = queries.astype(jnp.float32).reshape(block_count, block_rows, KVH, GROUP, HD)
    dout_all = out_grad.astype(jnp.float32).reshape(block_count, block_rows, KVH, GROUP, HD)
    row_dot = jnp.sum((out_grad.astype(jnp.float32) * outputs.astype(jnp.float32)).reshape(TOKENS, head_count, HD), -1)
    lse_all = log_sum_exp.reshape(block_count, block_rows, KVH, GROUP)
    dot_all = row_dot.reshape(block_count, block_rows, KVH, GROUP)
    key_heads = keys.astype(jnp.float32).reshape(TOKENS, KVH, HD)
    value_heads = values.astype(jnp.float32).reshape(TOKENS, KVH, HD)
    positions = jnp.arange(TOKENS, dtype=jnp.int32)
    pos_all = positions.reshape(block_count, block_rows)
    seg_all = segment_ids.reshape(block_count, block_rows)

    def visit(carried, items):
        grad_k, grad_v = carried
        query_blk, dout_blk, lse_blk, dot_blk, pos_blk, seg_blk = items
        visible = (positions[None, :] <= pos_blk[:, None]) & (segment_ids[None, :] == seg_blk[:, None])
        scores = jnp.einsum("qhgd,khd->hgqk", query_blk, key_heads) * scaling
        lse_t = jnp.transpose(lse_blk, (1, 2, 0))
        dot_t = jnp.transpose(dot_blk, (1, 2, 0))
        attn_probs = jnp.where(visible, jnp.exp(scores - lse_t[..., None]), 0.0)
        dprobs = jnp.einsum("qhgd,khd->hgqk", dout_blk, value_heads)
        dscores = attn_probs * (dprobs - dot_t[..., None])
        probs_half = lax.optimization_barrier(attn_probs.astype(jnp.bfloat16)).astype(jnp.float32)
        dscores_half = lax.optimization_barrier(dscores.astype(jnp.bfloat16)).astype(jnp.float32)
        grad_q = jnp.einsum("hgqk,khd->qhgd", dscores_half, key_heads) * scaling
        grad_k = grad_k + jnp.einsum("hgqk,qhgd->khd", dscores_half, query_blk) * scaling
        grad_v = grad_v + jnp.einsum("hgqk,qhgd->khd", probs_half, dout_blk)
        return (grad_k, grad_v), grad_q.reshape(block_rows, head_count * HD).astype(jnp.bfloat16)

    start_kv = (jnp.zeros((TOKENS, KVH, HD), jnp.float32), jnp.zeros((TOKENS, KVH, HD), jnp.float32))
    (grad_k, grad_v), grad_q = lax.scan(visit, start_kv, (query_all, dout_all, lse_all, dot_all, pos_all, seg_all))
    grad_queries = grad_q.reshape(TOKENS, head_count * HD)
    grad_keys = grad_k.reshape(TOKENS, KVH * HD).astype(jnp.bfloat16)
    grad_values = grad_v.reshape(TOKENS, KVH * HD).astype(jnp.bfloat16)
    return grad_queries, grad_keys, grad_values
```

```python
import functools
import math

import jax
import jax.numpy as jnp
from jax import lax
from jax.experimental import pallas as pl
from jax.experimental.pallas import tpu as pltpu
from jax.sharding import PartitionSpec as P

MESH = pl.DeviceIdType.MESH
HD = 128
GROUP = 4
NZ, NY, NX, NC = 8, 4, 4, 2
TOK = 128
PIECE = TOK // NZ
ROWS = PIECE * GROUP
NG = NZ * NY * NC
TILE_G = 4
NQT = NG // TILE_G
QT = TILE_G * ROWS
KT = 512
SUB = 128
ROUND = 96
BOTH = TOK - ROUND
NKEY = NZ * NX * TOK
NKT = NKEY // KT
CHUNK = NX * TOK
IDS = 72
STEPS = NQT * NKT + 4
SCALE = HD ** -0.5
LOG2E = math.log2(math.e)
BF = jnp.bfloat16
F32 = jnp.float32


def place():
    row = lax.axis_index("row")
    col = lax.axis_index("col")
    z = row // 4
    y = (row // 2) % 2 * 2 + col // 4
    return z, y, col % 4, row % 2


def device(z, y, x, c):
    return (z * 4 + y // 2 * 2 + c, y % 2 * 4 + x)


class Copies:
    def __init__(self, send, recv):
        self.send, self.recv, self.count, self.all = send, recv, 0, []

    def start(self, src, dst, to):
        i = self.count
        self.count += 1
        copy = pltpu.make_async_remote_copy(
            src_ref=src,
            dst_ref=dst,
            send_sem=self.send.at[i],
            recv_sem=self.recv.at[i],
            device_id=to,
            device_id_type=MESH,
        )
        copy.start()
        self.all.append(copy)
        return copy

    def finish(self):
        for copy in self.all:
            copy.wait_send()


def greet(peers):
    barrier = pltpu.get_barrier_semaphore()
    for peer in peers:
        pl.semaphore_signal(barrier, inc=1, device_id=peer, device_id_type=MESH)
    pl.semaphore_wait(barrier, len(peers))


N_GATHER = 32 + 7 + 7 + 7 + 24 + 4 + 11 + 10


def gather_kernel(
    q_in, k_in, v_in, o_in, do_in, lse_in, seg_in, kv_all, qd_all, st_all, sg_all,
    q_ref, o_ref, do_ref, lse_ref, seg_ref, qd_ref, st_ref, send, recv, local,
):
    z, y, x, c = place()
    xp, xm, xo = (x + 1) % NX, (x + 3) % NX, (x + 2) % NX
    yp, ym, yo = (y + 1) % NY, (y + 3) % NY, (y + 2) % NY
    zp, zm = (z + 1) % NZ, (z + NZ - 1) % NZ
    right, left, across = device(z, y, xp, c), device(z, y, xm, c), device(z, y, xo, c)
    up, down, beyond = device(z, yp, x, c), device(z, ym, x, c), device(z, yo, x, c)
    z_right, z_left = device(zp, y, x, c), device(zm, y, x, c)
    twin = device(z, y, x, 1 - c)
    planes = [(z + d) % NZ for d in range(1, NZ)]
    load = [
        pltpu.make_async_copy(src, dst, local.at[i])
        for i, (src, dst) in enumerate([
            (k_in, kv_all.at[z, x, :, pl.ds(0, HD)]),
            (v_in, kv_all.at[z, x, :, pl.ds(HD, HD)]),
            (q_in, q_ref),
            (do_in, do_ref),
            (o_in, o_ref),
            (lse_in, lse_ref),
            (seg_in, seg_ref),
        ])
    ]
    for copy in load:
        copy.start()
    greet(
        [right, left, across, up, down, beyond, twin] + [device(w, y, x, c) for w in planes]
    )
    copies = Copies(send, recv)
    start = copies.start
    yh, yl = y // 2, y % 2

    def spread(d):
        zb = (z + NZ + d) % NZ
        count = TOK if d == 0 else ROUND
        src = kv_all.at[zb, x, pl.ds(0, count)]
        near[d] = (start(src, src, right), start(src, src, left))

    def pass_on(d):
        zb = (z + NZ + d) % NZ
        count = (TOK if d == 0 else ROUND) // 2
        near[d][0].wait_recv()
        src = kv_all.at[zb, xm, pl.ds(0, count)]
        far[d] = [start(src, src, right)]
        near[d][1].wait_recv()
        src = kv_all.at[zb, xp, pl.ds(count, count)]
        far[d].append(start(src, src, left))

    def ring_a(s):
        if s > 0:
            hops["r", s].wait_recv()
        if s < 4:
            src = kv_all.at[(z + NZ - s) % NZ, x, pl.ds(0, ROUND)]
            hops["r", s + 1] = start(src, src, z_right)
        if 0 < s < 4:
            hops["l", s].wait_recv()
        if s < 3:
            src = kv_all.at[(z + s) % NZ, x, pl.ds(0, ROUND)]
            hops["l", s + 1] = start(src, src, z_left)

    def ring_b(s):
        if s > 0:
            hops["R", s].wait_recv()
        if s < 4:
            src = kv_all.at[(z + NZ - s) % NZ, :, pl.ds(ROUND, BOTH)]
            hops["R", s + 1] = start(src, src, z_right)
        if 0 < s < 4:
            hops["L", s].wait_recv()
        if s < 3:
            src = kv_all.at[(z + s) % NZ, :, pl.ds(ROUND, BOTH)]
            hops["L", s + 1] = start(src, src, z_left)

    def q_send(d):
        w = (z + NZ + d) % NZ
        pieces[d] = start(qd_ref.at[w], qd_all.at[z, yh, c, yl], device(w, y, x, c))

    def q_share(d):
        if d != 0:
            pieces[d].wait_recv()
        src = qd_all.at[(z + NZ - d) % NZ, yh, c, yl]
        q_near[d] = (start(src, src, up), start(src, src, down))

    def q_pass(d):
        zz = (z + NZ - d) % NZ
        q_near[d][0].wait_recv()
        q_near[d][1].wait_recv()
        if steps.index(d) % 2 == 0:
            src = qd_all.at[zz, ym // 2, c, ym % 2]
            q_far.append(start(src, src, up))
        else:
            src = qd_all.at[zz, yp // 2, c, yp % 2]
            q_far.append(start(src, src, down))

    def q_across(yy):
        src = qd_all.at[:, yy // 2, c, yy % 2]
        ends.append(start(src, src, twin))

    near, far, hops, pieces, q_near, q_far, ends = {}, {}, {}, {}, {}, [], []
    steps = [0, 1, -1, 2, -2, 3, -3, 4]
    load[0].wait()
    load[1].wait()
    spread(0)
    ring_a(0)
    load[2].wait()
    load[3].wait()
    for w in range(NZ):
        for h in range(GROUP):
            here = (slice(w * PIECE, (w + 1) * PIECE), slice(h * HD, (h + 1) * HD))
            there = slice(h * PIECE, (h + 1) * PIECE)
            qd_ref[w, 0, there] = q_ref[here]
            qd_ref[w, 1, there] = do_ref[here]
    for d in (1, -1, 2, -2):
        q_send(d)
    qd_all[z, yh, c, yl] = qd_ref[z]
    q_share(0)

    for copy in load[4:]:
        copy.wait()
    sub = lax.broadcasted_iota(jnp.int32, (TOK, TOK), 0)
    lane = lax.broadcasted_iota(jnp.int32, (TOK, TOK), 1)
    dots = []
    for h in range(GROUP):
        cols = slice(h * HD, (h + 1) * HD)
        both = lax.dot_general(
            do_ref[:, cols], o_ref[:, cols], (((1,), (1,)), ((), ())),
            preferred_element_type=F32,
        )
        dots.append(jnp.sum(jnp.where(sub == lane, both, 0.0), axis=0, keepdims=True))
    stats = jnp.concatenate([lse_ref[...]] + dots, axis=0)
    seg = seg_ref[...].astype(F32)
    sg_all[z, x] = seg
    segs = jnp.broadcast_to(seg, (2 * GROUP, TOK))
    sub, block = sub[0:8], lane[0:8] // PIECE
    turned = [
        [a if d == 0 else pltpu.roll(a, d * PIECE, 1) for d in range(NZ)] for a in (stats, segs)
    ]
    for w in range(NZ):
        for i in range(2):
            row = jnp.zeros((8, TOK), F32)
            for d in range(NZ):
                row += jnp.where((block == sub) & ((sub + NZ - w) % NZ == d), turned[i][d], 0.0)
            st_ref[w, i:i + 1, :] = jnp.sum(row, axis=0, keepdims=True)
    small = [
        start(st_ref.at[w], st_all.at[z, yh, c, yl], device(w, y, x, c)) for w in planes
    ]
    sg_ref = sg_all.at[z, x]
    marks = [start(sg_ref, sg_ref, device(w, y, x, c)) for w in planes]
    st_all[z, yh, c, yl] = st_ref[z]

    ring_a(1)
    spread(-1)
    spread(1)
    pass_on(0)
    ring_a(2)
    spread(-2)
    spread(2)
    for d in (3, -3, 4):
        q_send(d)
    for copy in far[0]:
        copy.wait_recv()
    ring_b(0)
    q_share(1)
    q_share(-1)
    pass_on(-1)
    ring_a(3)
    spread(-3)
    spread(3)
    pass_on(1)
    q_share(2)
    q_share(-2)
    q_pass(0)
    q_pass(1)
    ring_b(1)
    pass_on(-2)
    ring_a(4)
    spread(-4)
    q_pass(-1)
    for copy in small + marks:
        copy.wait_recv()
    few = st_all.at[:, yh, c, yl]
    st_y = [start(few, few, to) for to in (up, down, beyond)]
    few = sg_all.at[:, x]
    sg_x = [start(few, few, to) for to in (right, left, across)]
    pass_on(2)
    q_share(3)
    q_share(-3)
    q_share(4)
    q_across(y)
    ring_b(2)
    q_pass(2)
    q_pass(-2)
    pass_on(-3)
    for copy in st_y:
        copy.wait_recv()
    few = st_all.at[:, :, c]
    ends.append(start(few, few, twin))
    pass_on(3)
    ring_b(3)
    q_pass(3)
    q_pass(-3)
    q_pass(4)
    q_across(yp)
    q_across(ym)
    pass_on(-4)
    for copy in q_far:
        copy.wait_recv()
    q_across(yo)
    ring_b(4)
    for d in steps[1:]:
        for copy in far[-d]:
            copy.wait_recv()
    for copy in sg_x + ends:
        copy.wait_recv()
    assert copies.count == N_GATHER, copies.count
    copies.finish()


def attend_kernel(
    kv_ref, qd_ref, st_ref, sg_ref, dkv_ref, dq_ref,
    rows_ref, dq_acc, dk_acc, dv_acc, keys_t, p_ref, ds_ref,
    low_ref, k_list, t_list, from_list,
):
    z, y, x, c = place()
    key_start = y // 2 * 2048 + c * 1024 + y % 2 * 512
    query_start = x * TOK + z * PIECE

    ids = lax.broadcasted_iota(jnp.int32, (IDS, TOK), 0).astype(F32)
    before = jnp.zeros((IDS, TOK), F32)
    for b in range(NZ * NX):
        before += jnp.where(sg_ref[b] < ids, 1.0, 0.0)
    before = jnp.sum(before, axis=1, keepdims=True)
    id_col = lax.broadcasted_iota(jnp.int32, (IDS, QT), 0).astype(F32)
    lane = lax.broadcasted_iota(jnp.int32, (1, 128), 1)
    lane_q = lax.broadcasted_iota(jnp.int32, (1, QT), 1)
    half = lane < ROWS

    for t in range(NQT):
        g = t * TILE_G
        stats = [st_ref[g + i, 0:1, :] for i in range(TILE_G)]
        turned = [pltpu.roll(s, ROWS, 1) for s in stats]
        lse = jnp.concatenate(
            [jnp.where(half, stats[0], turned[1]), jnp.where(half, stats[2], turned[3])], axis=1
        )
        dot = jnp.concatenate(
            [jnp.where(half, turned[0], stats[1]), jnp.where(half, turned[2], stats[3])], axis=1
        )
        seg = [st_ref[g + i, 1:2, :] for i in range(TILE_G)]
        seg = jnp.concatenate(
            [jnp.where(half, seg[0], seg[1]), jnp.where(half, seg[2], seg[3])], axis=1
        )
        lo = jnp.sum(jnp.where(id_col == seg, before, 0.0), axis=0, keepdims=True)
        piece = g + lane_q // ROWS
        rem = piece % NZ * CHUNK + query_start + lane_q % PIECE - key_start
        hi = piece // NZ * CHUNK + jnp.clip(rem + 1, 0, CHUNK)
        rows_ref[t, 0:1, :] = lse * LOG2E
        rows_ref[t, 1:2, :] = dot
        rows_ref[t, 2:3, :] = lo
        rows_ref[t, 3:4, :] = hi.astype(F32)
        low_ref[t] = jnp.min(lo).astype(jnp.int32)

    def clear(k, carry):
        dq_acc[2 * k] = jnp.zeros((HD, QT), F32)
        dq_acc[2 * k + 1] = jnp.zeros((HD, QT), F32)
        dk_acc[k] = jnp.zeros((KT, HD), F32)
        dv_acc[k] = jnp.zeros((KT, HD), F32)
        keys_t[k] = kv_ref[k, :, 0:HD].T
        return carry

    lax.fori_loop(0, NKT, clear, 0)
    p_ref[...] = jnp.zeros((KT, QT), BF)
    ds_ref[...] = jnp.zeros((KT, QT), BF)

    def nothing(n):
        k_list[n] = 0
        t_list[n] = 0
        from_list[n] = -(1 << 20)

    nothing(0)

    def listed(k, count):
        ahead = k * (NZ * CHUNK) + key_start - query_start - (PIECE - 1)
        for t in range(NQT):
            k_list[count] = k
            t_list[count] = t
            from_list[count] = k * KT
            seen = (low_ref[t] < (k + 1) * KT) & (ahead <= (t * TILE_G + TILE_G - 1) * CHUNK)
            count += jnp.where(seen, 1, 0)
        return count

    count = lax.fori_loop(0, NKT, listed, 1)
    nothing(count)

    def step(n, carry):
        k, t = k_list[n], t_list[n]
        q = qd_ref[pl.ds(t * TILE_G, TILE_G), 0].reshape(QT, HD)
        do = qd_ref[pl.ds(t * TILE_G, TILE_G), 1].reshape(QT, HD)
        p, ds = p_ref[...], ds_ref[...]
        dv_acc[k] += jnp.dot(p, do, preferred_element_type=F32)
        dk_acc[k] += jnp.dot(ds, q, preferred_element_type=F32)
        dq_acc[t] += jnp.dot(keys_t[k], ds, preferred_element_type=F32)
        k, t = k_list[n + 1], t_list[n + 1]
        q = qd_ref[pl.ds(t * TILE_G, TILE_G), 0].reshape(QT, HD)
        do = qd_ref[pl.ds(t * TILE_G, TILE_G), 1].reshape(QT, HD)
        start = from_list[n + 1].astype(F32)
        low = rows_ref[t, 2:3, :] - start
        high = rows_ref[t, 3:4, :] - start
        across = (((1,), (1,)), ((), ()))
        for i in range(KT // SUB):
            part = pl.ds(i * SUB, SUB)
            s = lax.dot_general(kv_ref[k, part, 0:HD], q, across, preferred_element_type=F32)
            dp = lax.dot_general(
                kv_ref[k, part, HD:2 * HD], do, across, preferred_element_type=F32
            )
            index = (lax.broadcasted_iota(jnp.int32, (SUB, QT), 0) + i * SUB).astype(F32)
            seen = (index >= low) & (index < high)
            p = jnp.where(seen, jnp.exp2(s * (SCALE * LOG2E) - rows_ref[t, 0:1, :]), 0.0)
            p_ref[part, :] = p.astype(BF)
            ds_ref[part, :] = (p * (dp - rows_ref[t, 1:2, :])).astype(BF)
        return carry

    lax.fori_loop(0, count, step, 0)

    def emit(k, carry):
        dkv_ref[k, :, 0:HD] = (dk_acc[k] * SCALE).astype(BF)
        dkv_ref[k, :, HD:2 * HD] = dv_acc[k].astype(BF)
        for i in range(NQT // NKT):
            t = k * (NQT // NKT) + i
            dq = (dq_acc[t] * SCALE).T
            dq_ref[pl.ds(t * TILE_G, TILE_G)] = dq.astype(BF).reshape(TILE_G, ROWS, HD)
        return carry

    lax.fori_loop(0, NKT, emit, 0)


N_REDUCE = 16 + 16 + 7 + 7 + 4 + 1 + 2 + 2 + 7


def reduce_kernel(
    kv_ref, dq_in, gq_ref, gk_ref, gv_ref,
    far, near, out_x, ring_in, ring_out, both_in, both_out, both_sum, b_far, b_near, b_out,
    q_twin, q_sum, q_far, q_near, q_out, q_send, q_back, send, recv,
):
    z, y, x, c = place()
    xp, xm, xo = (x + 1) % NX, (x + 3) % NX, (x + 2) % NX
    yp, ym, yo = (y + 1) % NY, (y + 3) % NY, (y + 2) % NY
    zp, zm = (z + 1) % NZ, (z + NZ - 1) % NZ
    right, left = device(z, y, xp, c), device(z, y, xm, c)
    up, down = device(z, yp, x, c), device(z, ym, x, c)
    z_right, z_left = device(zp, y, x, c), device(zm, y, x, c)
    twin = device(z, y, x, 1 - c)
    planes = [(z + d) % NZ for d in range(1, NZ)]
    greet([right, left, up, down, twin] + [device(w, y, x, c) for w in planes])
    copies = Copies(send, recv)
    start = copies.start
    h = ROUND // 2
    rest = pl.ds(ROUND, BOTH)
    order = [4, 3, -3, 2, -2, 1, -1, 0]

    def first(n):
        zb = (z + NZ + order[n]) % NZ
        return (
            start(kv_ref.at[zb, xo, pl.ds(0, h)], far.at[n, 0], right),
            start(kv_ref.at[zb, xo, pl.ds(h, h)], far.at[n, 1], left),
        )

    def second(n, pair):
        zb = (z + NZ + order[n]) % NZ
        pair[0].wait_recv()
        out_x[n, 0, 0:h] = (kv_ref[zb, xp, 0:h].astype(F32) + far[n, 0].astype(F32)).astype(BF)
        out_x[n, 0, h:ROUND] = kv_ref[zb, xp, h:ROUND]
        a = start(out_x.at[n, 0], near.at[n, 0], right)
        pair[1].wait_recv()
        out_x[n, 1, 0:h] = kv_ref[zb, xm, 0:h]
        out_x[n, 1, h:ROUND] = (kv_ref[zb, xm, h:ROUND].astype(F32) + far[n, 1].astype(F32)).astype(BF)
        b = start(out_x.at[n, 1], near.at[n, 1], left)
        return a, b

    ring = {}

    def third(n, pair):
        off = order[n]
        zb = (z + NZ + off) % NZ
        pair[0].wait_recv()
        pair[1].wait_recv()
        total = kv_ref[zb, x, 0:ROUND].astype(F32) + near[n, 0].astype(F32) + near[n, 1].astype(F32)
        if off > 0:
            hop = 4 - off
            if hop > 0:
                ring[("r", hop)].wait_recv()
                total += ring_in[hop - 1].astype(F32)
            ring_out[n] = total.astype(BF)
            ring[("r", hop + 1)] = start(ring_out.at[n], ring_in.at[hop], z_right)
        elif off < 0:
            hop = 3 + off
            if hop > 0:
                ring[("l", hop)].wait_recv()
                total += ring_in[4 + hop - 1].astype(F32)
            ring_out[n] = total.astype(BF)
            ring[("l", hop + 1)] = start(ring_out.at[n], ring_in.at[4 + hop], z_left)
        else:
            ring[("r", 4)].wait_recv()
            ring[("l", 3)].wait_recv()
            total += ring_in[3].astype(F32) + ring_in[6].astype(F32)
            gk_ref[0:ROUND] = total[:, 0:HD].astype(BF)
            gv_ref[0:ROUND] = total[:, HD:2 * HD].astype(BF)

    def both(s):
        if s == 0:
            ring["R", 1] = start(kv_ref.at[(z + 4) % NZ, :, rest], both_in.at[0], z_right)
            ring["L", 1] = start(kv_ref.at[(z + 5) % NZ, :, rest], both_in.at[4], z_left)
            return
        if s < 5:
            ring["R", s].wait_recv()
        if s < 4:
            mine = kv_ref[(z + 4 - s) % NZ, :, ROUND:TOK].astype(F32)
            both_out[s - 1] = (mine + both_in[s - 1].astype(F32)).astype(BF)
            ring["R", s + 1] = start(both_out.at[s - 1], both_in.at[s], z_right)
        if s < 3:
            ring["L", s].wait_recv()
            mine = kv_ref[(z + 5 + s) % NZ, :, ROUND:TOK].astype(F32)
            both_out[2 + s] = (mine + both_in[3 + s].astype(F32)).astype(BF)
            ring["L", s + 1] = start(both_out.at[2 + s], both_in.at[4 + s], z_left)
        if s == 4:
            ring["L", 3].wait_recv()
            both_sum[...] = (
                kv_ref[z, :, ROUND:TOK].astype(F32)
                + both_in[3].astype(F32)
                + both_in[6].astype(F32)
            ).astype(BF)
            b = BOTH // 2
            ring["f", 0] = start(both_sum.at[xo, pl.ds(0, b)], b_far.at[0], right)
            ring["f", 1] = start(both_sum.at[xo, pl.ds(b, b)], b_far.at[1], left)
        if s == 5:
            b = BOTH // 2
            ring["f", 0].wait_recv()
            b_out[0, 0:b] = (both_sum[xp, 0:b].astype(F32) + b_far[0].astype(F32)).astype(BF)
            b_out[0, b:BOTH] = both_sum[xp, b:BOTH]
            ring["n", 0] = start(b_out.at[0], b_near.at[0], right)
            ring["f", 1].wait_recv()
            b_out[1, 0:b] = both_sum[xm, 0:b]
            b_out[1, b:BOTH] = (both_sum[xm, b:BOTH].astype(F32) + b_far[1].astype(F32)).astype(BF)
            ring["n", 1] = start(b_out.at[1], b_near.at[1], left)

    def both_end():
        ring["n", 0].wait_recv()
        ring["n", 1].wait_recv()
        total = both_sum[x].astype(F32) + b_near[0].astype(F32) + b_near[1].astype(F32)
        gk_ref[ROUND:TOK] = total[:, 0:HD].astype(BF)
        gv_ref[ROUND:TOK] = total[:, HD:2 * HD].astype(BF)

    swap = start(dq_in.at[:, :, 1 - c], q_twin, twin)
    both(0)
    one = [first(0), first(1)]
    two = []
    for n in range(NZ):
        if n + 2 < NZ:
            one.append(first(n + 2))
        two.append(second(n, one[n]))
        if n == 0:
            swap.wait_recv()
            for zz in range(NZ):
                q_sum[zz] = (dq_in[zz, :, c].astype(F32) + q_twin[zz].astype(F32)).astype(BF)
            q_a = start(q_sum.at[pl.ds(0, 4), yo // 2, yo % 2], q_far.at[0], up)
            q_b = start(q_sum.at[pl.ds(4, 4), yo // 2, yo % 2], q_far.at[1], down)
        if n in (1, 3, 5):
            both(n // 2 + 1)
        if n > 5:
            both(n - 2)
        if n > 0:
            third(n - 1, two[n - 1])
        if n == 2:
            q_a.wait_recv()
            q_out[0, 0:4] = (
                q_sum[0:4, yp // 2, yp % 2].astype(F32) + q_far[0].astype(F32)
            ).astype(BF)
            q_out[0, 4:8] = q_sum[4:8, yp // 2, yp % 2]
            q_c = start(q_out.at[0], q_near.at[0], up)
            q_b.wait_recv()
            q_out[1, 0:4] = q_sum[0:4, ym // 2, ym % 2]
            q_out[1, 4:8] = (
                q_sum[4:8, ym // 2, ym % 2].astype(F32) + q_far[1].astype(F32)
            ).astype(BF)
            q_d = start(q_out.at[1], q_near.at[1], down)
        if n == 5:
            q_c.wait_recv()
            q_d.wait_recv()
            q_send[...] = (
                q_sum[:, y // 2, y % 2].astype(F32)
                + q_near[0].astype(F32)
                + q_near[1].astype(F32)
            ).astype(BF)
            back = [start(q_send.at[w], q_back.at[z], device(w, y, x, c)) for w in planes]
            q_back[z] = q_send[z]
    third(NZ - 1, two[NZ - 1])
    both_end()
    for copy in back:
        copy.wait_recv()
    for w in range(NZ):
        for head in range(GROUP):
            gq_ref[w * PIECE:(w + 1) * PIECE, head * HD:(head + 1) * HD] = q_back[
                w, head * PIECE:(head + 1) * PIECE
            ]
    assert copies.count == N_REDUCE, copies.count
    copies.finish()


def body(queries, keys, values, outputs, out_grad, log_sum_exp, segment_ids):
    hbm = pl.BlockSpec(memory_space=pltpu.HBM)
    vmem = pl.BlockSpec(memory_space=pltpu.VMEM)

    kv_all, qd_all, st_all, sg_all = pl.pallas_call(
        gather_kernel,
        out_shape=[
            jax.ShapeDtypeStruct((NZ, NX, TOK, 2 * HD), BF),
            jax.ShapeDtypeStruct((NZ, 2, NC, 2, 2, ROWS, HD), BF),
            jax.ShapeDtypeStruct((NZ, 2, NC, 2, 2, 128), F32),
            jax.ShapeDtypeStruct((NZ, NX, 1, TOK), F32),
        ],
        in_specs=[hbm] * 7,
        out_specs=[vmem] * 4,
        scratch_shapes=[
            pltpu.VMEM((TOK, GROUP * HD), BF),
            pltpu.VMEM((TOK, GROUP * HD), BF),
            pltpu.VMEM((TOK, GROUP * HD), BF),
            pltpu.VMEM((GROUP, TOK), F32),
            pltpu.VMEM((1, TOK), jnp.int32),
            pltpu.VMEM((NZ, 2, ROWS, HD), BF),
            pltpu.VMEM((NZ, 2, 2 * ROWS), F32),
            pltpu.SemaphoreType.DMA((N_GATHER,)),
            pltpu.SemaphoreType.DMA((N_GATHER,)),
            pltpu.SemaphoreType.DMA((7,)),
        ],
        compiler_params=pltpu.CompilerParams(
            collective_id=0, has_side_effects=True, vmem_limit_bytes=40 * 2**20
        ),
        name="gather",
    )(
        *[
            pltpu.with_memory_space_constraint(a, pltpu.HBM)
            for a in (
                queries, keys, values, outputs, out_grad,
                log_sum_exp.T, segment_ids.reshape(1, TOK),
            )
        ]
    )

    dkv, dq = pl.pallas_call(
        attend_kernel,
        out_shape=[
            jax.ShapeDtypeStruct((NKT, KT, 2 * HD), BF),
            jax.ShapeDtypeStruct((NG, ROWS, HD), BF),
        ],
        in_specs=[vmem] * 4,
        out_specs=[vmem] * 2,
        scratch_shapes=[
            pltpu.VMEM((NQT, 8, QT), F32),
            pltpu.VMEM((NQT, HD, QT), F32),
            pltpu.VMEM((NKT, KT, HD), F32),
            pltpu.VMEM((NKT, KT, HD), F32),
            pltpu.VMEM((NKT, HD, KT), BF),
            pltpu.VMEM((KT, QT), BF),
            pltpu.VMEM((KT, QT), BF),
            pltpu.SMEM((NQT,), jnp.int32),
            pltpu.SMEM((STEPS,), jnp.int32),
            pltpu.SMEM((STEPS,), jnp.int32),
            pltpu.SMEM((STEPS,), jnp.int32),
        ],
        compiler_params=pltpu.CompilerParams(vmem_limit_bytes=40 * 2**20),
        name="attend",
    )(
        kv_all.reshape(NKT, KT, 2 * HD),
        qd_all.reshape(NG, 2, ROWS, HD),
        st_all.reshape(NG, 2, 128),
        sg_all.reshape(NZ * NX, 1, TOK),
    )

    return pl.pallas_call(
        reduce_kernel,
        out_shape=[
            jax.ShapeDtypeStruct((TOK, GROUP * HD), BF),
            jax.ShapeDtypeStruct((TOK, HD), BF),
            jax.ShapeDtypeStruct((TOK, HD), BF),
        ],
        in_specs=[vmem] * 2,
        out_specs=[vmem] * 3,
        scratch_shapes=[
            pltpu.VMEM((NZ, 2, ROUND // 2, 2 * HD), BF),
            pltpu.VMEM((NZ, 2, ROUND, 2 * HD), BF),
            pltpu.VMEM((NZ, 2, ROUND, 2 * HD), BF),
            pltpu.VMEM((7, ROUND, 2 * HD), BF),
            pltpu.VMEM((7, ROUND, 2 * HD), BF),
            pltpu.VMEM((7, NX, BOTH, 2 * HD), BF),
            pltpu.VMEM((5, NX, BOTH, 2 * HD), BF),
            pltpu.VMEM((NX, BOTH, 2 * HD), BF),
            pltpu.VMEM((2, BOTH // 2, 2 * HD), BF),
            pltpu.VMEM((2, BOTH, 2 * HD), BF),
            pltpu.VMEM((2, BOTH, 2 * HD), BF),
            pltpu.VMEM((NZ, 2, 2, ROWS, HD), BF),
            pltpu.VMEM((NZ, 2, 2, ROWS, HD), BF),
            pltpu.VMEM((2, 4, ROWS, HD), BF),
            pltpu.VMEM((2, NZ, ROWS, HD), BF),
            pltpu.VMEM((2, NZ, ROWS, HD), BF),
            pltpu.VMEM((NZ, ROWS, HD), BF),
            pltpu.VMEM((NZ, ROWS, HD), BF),
            pltpu.SemaphoreType.DMA((N_REDUCE,)),
            pltpu.SemaphoreType.DMA((N_REDUCE,)),
        ],
        compiler_params=pltpu.CompilerParams(
            collective_id=1, has_side_effects=True, vmem_limit_bytes=40 * 2**20
        ),
        name="reduce",
    )(
        dkv.reshape(NZ, NX, TOK, 2 * HD),
        dq.reshape(NZ, 2, NC, 2, ROWS, HD),
    )


def solution(mesh):
    rows = P(("row", "col"), None)
    return jax.shard_map(
        body,
        mesh=mesh,
        in_specs=(rows, rows, rows, rows, rows, rows, P(("row", "col"))),
        out_specs=(rows, rows, rows),
        check_vma=False,
    )
```

```python
import functools
import math

import jax
import jax.numpy as jnp
from jax import lax
from jax.experimental import pallas as pl
from jax.experimental.pallas import tpu as pltpu
from jax.sharding import PartitionSpec as P

MESH = pl.DeviceIdType.MESH
HD = 128
GROUP = 4
NZ, NY, NX, NC = 8, 4, 4, 2
TOK = 128
PIECE = TOK // NZ
ROWS = PIECE * GROUP
NG = NZ * NY * NC
TILE_G = 4
NQT = NG // TILE_G
QT = TILE_G * ROWS
KT = 512
SUB = 128
ROUND = 96
BOTH = TOK - ROUND
NKEY = NZ * NX * TOK
NKT = NKEY // KT
CHUNK = NX * TOK
IDS = 72
STEPS = NQT * NKT + 4
SCALE = HD ** -0.5
LOG2E = math.log2(math.e)
BF = jnp.bfloat16
F32 = jnp.float32


def place():
    row = lax.axis_index("row")
    col = lax.axis_index("col")
    z = row // 4
    y = (row // 2) % 2 * 2 + col // 4
    return z, y, col % 4, row % 2


def device(z, y, x, c):
    return (z * 4 + y // 2 * 2 + c, y % 2 * 4 + x)


class Copies:
    def __init__(self, send, recv):
        self.send, self.recv, self.count, self.all = send, recv, 0, []

    def start(self, src, dst, to):
        i = self.count
        self.count += 1
        copy = pltpu.make_async_remote_copy(
            src_ref=src,
            dst_ref=dst,
            send_sem=self.send.at[i],
            recv_sem=self.recv.at[i],
            device_id=to,
            device_id_type=MESH,
        )
        copy.start()
        self.all.append(copy)
        return copy

    def finish(self):
        for copy in self.all:
            copy.wait_send()


def greet(peers):
    barrier = pltpu.get_barrier_semaphore()
    for peer in peers:
        pl.semaphore_signal(barrier, inc=1, device_id=peer, device_id_type=MESH)
    pl.semaphore_wait(barrier, len(peers))


N_GATHER = 32 + 7 + 7 + 24 + 4 + 11 + 10


def gather_kernel(
    q_in, k_in, v_in, o_in, do_in, lse_in, seg_in, kv_all, qd_all, st_all, sg_all,
    q_ref, o_ref, do_ref, lse_ref, seg_ref, qd_ref, st_ref, send, recv, local,
):
    z, y, x, c = place()
    xp, xm, xo = (x + 1) % NX, (x + 3) % NX, (x + 2) % NX
    yp, ym, yo = (y + 1) % NY, (y + 3) % NY, (y + 2) % NY
    zp, zm = (z + 1) % NZ, (z + NZ - 1) % NZ
    right, left, across = device(z, y, xp, c), device(z, y, xm, c), device(z, y, xo, c)
    up, down, beyond = device(z, yp, x, c), device(z, ym, x, c), device(z, yo, x, c)
    z_right, z_left = device(zp, y, x, c), device(zm, y, x, c)
    twin = device(z, y, x, 1 - c)
    planes = [(z + d) % NZ for d in range(1, NZ)]
    load = [
        pltpu.make_async_copy(src, dst, local.at[i])
        for i, (src, dst) in enumerate([
            (k_in, kv_all.at[z, x, :, pl.ds(0, HD)]),
            (v_in, kv_all.at[z, x, :, pl.ds(HD, HD)]),
            (q_in, q_ref),
            (do_in, do_ref),
            (o_in, o_ref),
            (lse_in, lse_ref),
            (seg_in, seg_ref),
        ])
    ]
    for copy in load:
        copy.start()
    greet(
        [right, left, across, up, down, beyond, twin] + [device(w, y, x, c) for w in planes]
    )
    copies = Copies(send, recv)
    start = copies.start
    yh, yl = y // 2, y % 2

    near, far, hops, pieces, q_near, q_far = {}, {}, {}, {}, {}, []
    few, ends = {}, []
    steps = [0, 1, -1, 2, -2, 3, -3, 4]
    h = TOK // 2

    def ring(s):
        if s > 0:
            hops["r", s].wait_recv()
        if s < 4:
            src = kv_all.at[(z + NZ - s) % NZ, x]
            hops["r", s + 1] = start(src, src, z_right)
        if 0 < s < 4:
            hops["l", s].wait_recv()
        if s < 3:
            src = kv_all.at[(z + s) % NZ, x]
            hops["l", s + 1] = start(src, src, z_left)

    def spread(d):
        src = kv_all.at[(z + NZ + d) % NZ, x]
        near[d] = (start(src, src, right), start(src, src, left))

    def pass_on(d):
        zb = (z + NZ + d) % NZ
        near[d][0].wait_recv()
        src = kv_all.at[zb, xm, pl.ds(0, h)]
        far[d] = [start(src, src, right)]
        near[d][1].wait_recv()
        src = kv_all.at[zb, xp, pl.ds(h, h)]
        far[d].append(start(src, src, left))

    def pack(_):
        load[2].wait()
        load[3].wait()
        for w in range(NZ):
            for g in range(GROUP):
                here = (slice(w * PIECE, (w + 1) * PIECE), slice(g * HD, (g + 1) * HD))
                there = slice(g * PIECE, (g + 1) * PIECE)
                qd_ref[w, 0, there] = q_ref[here]
                qd_ref[w, 1, there] = do_ref[here]
        qd_all[z, yh, c, yl] = qd_ref[z]

    def q_send(d):
        w = (z + NZ + d) % NZ
        pieces[d] = start(qd_ref.at[w], qd_all.at[z, yh, c, yl], device(w, y, x, c))

    def q_share(d):
        if d != 0:
            pieces[d].wait_recv()
        src = qd_all.at[(z + NZ - d) % NZ, yh, c, yl]
        q_near[d] = (start(src, src, up), start(src, src, down))

    def q_pass(d):
        zz = (z + NZ - d) % NZ
        q_near[d][0].wait_recv()
        q_near[d][1].wait_recv()
        if steps.index(d) % 2 == 0:
            src = qd_all.at[zz, ym // 2, c, ym % 2]
            q_far.append(start(src, src, up))
        else:
            src = qd_all.at[zz, yp // 2, c, yp % 2]
            q_far.append(start(src, src, down))

    def q_across(where):
        if where == 2:
            for copy in q_far:
                copy.wait_recv()
        for yy in ((y,), (yp, ym), (yo,))[where]:
            src = qd_all.at[:, yy // 2, c, yy % 2]
            ends.append(start(src, src, twin))

    def stats(stage):
        if stage == 0:
            for copy in load[4:]:
                copy.wait()
            sub = lax.broadcasted_iota(jnp.int32, (TOK, TOK), 0)
            lane = lax.broadcasted_iota(jnp.int32, (TOK, TOK), 1)
            dots = []
            for g in range(GROUP):
                cols = slice(g * HD, (g + 1) * HD)
                both = lax.dot_general(
                    do_ref[:, cols], o_ref[:, cols], (((1,), (1,)), ((), ())),
                    preferred_element_type=F32,
                )
                dots.append(jnp.sum(jnp.where(sub == lane, both, 0.0), axis=0, keepdims=True))
            numbers = jnp.concatenate([lse_ref[...]] + dots, axis=0)
            seg = seg_ref[...].astype(F32)
            sg_all[z, x] = seg
            segs = jnp.broadcast_to(seg, (2 * GROUP, TOK))
            sub, block = sub[0:8], lane[0:8] // PIECE
            turned = [
                [a if d == 0 else pltpu.roll(a, d * PIECE, 1) for d in range(NZ)]
                for a in (numbers, segs)
            ]
            for w in range(NZ):
                for i in range(2):
                    row = jnp.zeros((8, TOK), F32)
                    for d in range(NZ):
                        fits = (block == sub) & ((sub + NZ - w) % NZ == d)
                        row += jnp.where(fits, turned[i][d], 0.0)
                    st_ref[w, i:i + 1, :] = jnp.sum(row, axis=0, keepdims=True)
            st_all[z, yh, c, yl] = st_ref[z]
            few[0] = [
                start(st_ref.at[w], st_all.at[z, yh, c, yl], device(w, y, x, c)) for w in planes
            ]
            src = sg_all.at[z, x]
            few[0] += [start(src, src, device(w, y, x, c)) for w in planes]
        elif stage == 1:
            for copy in few[0]:
                copy.wait_recv()
            src = st_all.at[:, yh, c, yl]
            few[1] = [start(src, src, to) for to in (up, down, beyond)]
            src = sg_all.at[:, x]
            ends.extend([start(src, src, to) for to in (right, left, across)])
        else:
            for copy in few[1]:
                copy.wait_recv()
            src = st_all.at[:, :, c]
            ends.append(start(src, src, twin))

    load[0].wait()
    load[1].wait()
    for do, which in [
        (spread, 0), (ring, 0), (pack, 0), (q_send, 2), (q_send, 1), (q_send, -3), (ring, 1),
        (spread, -1), (spread, 1), (q_send, 4), (q_send, -1), (q_send, -2), (stats, 0),
        (pass_on, -1), (ring, 2), (q_share, 1), (spread, 2), (spread, -2), (q_share, 0),
        (pass_on, 1), (q_share, -3), (q_send, 3), (q_share, -2), (q_share, 2), (pass_on, 2),
        (q_share, 4), (q_share, -1), (ring, 3), (q_pass, -3), (spread, 3), (q_pass, 2),
        (spread, -3), (stats, 1), (q_share, 3), (q_pass, 4), (q_pass, -2), (pass_on, -2),
        (q_pass, 0), (ring, 4), (spread, -4), (q_pass, 1), (q_across, 0), (q_pass, -1),
        (q_pass, 3), (q_across, 1), (pass_on, 3), (pass_on, 0), (stats, 2), (pass_on, -3),
        (pass_on, -4), (q_across, 2),
    ]:
        do(which)
    for d in far:
        for copy in far[d]:
            copy.wait_recv()
    for copy in ends:
        copy.wait_recv()
    assert copies.count == N_GATHER, copies.count
    copies.finish()


def attend_kernel(
    kv_ref, qd_ref, st_ref, sg_ref, dkv_ref, dq_ref,
    rows_ref, dq_acc, dk_acc, dv_acc, keys_t, p_ref, ds_ref,
    low_ref, high_ref, k_list, t_list, from_list, full_list,
):
    z, y, x, c = place()
    key_start = y // 2 * 2048 + c * 1024 + y % 2 * 512
    query_start = x * TOK + z * PIECE

    ids = lax.broadcasted_iota(jnp.int32, (IDS, TOK), 0).astype(F32)
    before = jnp.zeros((IDS, TOK), F32)
    for b in range(NZ * NX):
        before += jnp.where(sg_ref[b] < ids, 1.0, 0.0)
    before = jnp.sum(before, axis=1, keepdims=True)
    id_col = lax.broadcasted_iota(jnp.int32, (IDS, QT), 0).astype(F32)
    lane = lax.broadcasted_iota(jnp.int32, (1, 128), 1)
    lane_q = lax.broadcasted_iota(jnp.int32, (1, QT), 1)
    half = lane < ROWS

    for t in range(NQT):
        g = t * TILE_G
        stats = [st_ref[g + i, 0:1, :] for i in range(TILE_G)]
        turned = [pltpu.roll(s, ROWS, 1) for s in stats]
        lse = jnp.concatenate(
            [jnp.where(half, stats[0], turned[1]), jnp.where(half, stats[2], turned[3])], axis=1
        )
        dot = jnp.concatenate(
            [jnp.where(half, turned[0], stats[1]), jnp.where(half, turned[2], stats[3])], axis=1
        )
        seg = [st_ref[g + i, 1:2, :] for i in range(TILE_G)]
        seg = jnp.concatenate(
            [jnp.where(half, seg[0], seg[1]), jnp.where(half, seg[2], seg[3])], axis=1
        )
        lo = jnp.sum(jnp.where(id_col == seg, before, 0.0), axis=0, keepdims=True)
        piece = g + lane_q // ROWS
        rem = piece % NZ * CHUNK + query_start + lane_q % PIECE - key_start
        hi = piece // NZ * CHUNK + jnp.clip(rem + 1, 0, CHUNK)
        rows_ref[t, 0:1, :] = lse * LOG2E
        rows_ref[t, 1:2, :] = dot
        rows_ref[t, 2:3, :] = lo
        rows_ref[t, 3:4, :] = hi.astype(F32)
        low_ref[t] = jnp.min(lo).astype(jnp.int32)
        high_ref[t] = jnp.max(lo).astype(jnp.int32)

    def clear(k, carry):
        dq_acc[2 * k] = jnp.zeros((HD, QT), F32)
        dq_acc[2 * k + 1] = jnp.zeros((HD, QT), F32)
        dk_acc[k] = jnp.zeros((KT, HD), F32)
        dv_acc[k] = jnp.zeros((KT, HD), F32)
        keys_t[k] = kv_ref[k, :, 0:HD].T
        return carry

    lax.fori_loop(0, NKT, clear, 0)
    p_ref[...] = jnp.zeros((KT, QT), BF)
    ds_ref[...] = jnp.zeros((KT, QT), BF)

    def nothing(n):
        k_list[n] = 0
        t_list[n] = 0
        from_list[n] = -(1 << 20)
        full_list[n] = 0

    nothing(0)

    def listed(k, count):
        ahead = k * (NZ * CHUNK) + key_start - query_start - (PIECE - 1)
        for t in range(NQT):
            k_list[count] = k
            t_list[count] = t
            from_list[count] = k * KT
            whole = (high_ref[t] <= k * KT) & (
                k * (NZ * CHUNK) + key_start + KT - 1 <= t * TILE_G * CHUNK + query_start
            )
            full_list[count] = jnp.where(whole, 1, 0)
            seen = (low_ref[t] < (k + 1) * KT) & (ahead <= (t * TILE_G + TILE_G - 1) * CHUNK)
            count += jnp.where(seen, 1, 0)
        return count

    count = lax.fori_loop(0, NKT, listed, 1)
    nothing(count)

    def work(n, masked):
        k, t = k_list[n], t_list[n]
        q = qd_ref[pl.ds(t * TILE_G, TILE_G), 0].reshape(QT, HD)
        do = qd_ref[pl.ds(t * TILE_G, TILE_G), 1].reshape(QT, HD)
        p, ds = p_ref[...], ds_ref[...]
        dv_acc[k] += jnp.dot(p, do, preferred_element_type=F32)
        dk_acc[k] += jnp.dot(ds, q, preferred_element_type=F32)
        dq_acc[t] += jnp.dot(keys_t[k], ds, preferred_element_type=F32)
        k, t = k_list[n + 1], t_list[n + 1]
        q = qd_ref[pl.ds(t * TILE_G, TILE_G), 0].reshape(QT, HD)
        do = qd_ref[pl.ds(t * TILE_G, TILE_G), 1].reshape(QT, HD)
        start = from_list[n + 1].astype(F32)
        low = rows_ref[t, 2:3, :] - start
        high = rows_ref[t, 3:4, :] - start
        across = (((1,), (1,)), ((), ()))
        for i in range(KT // SUB):
            part = pl.ds(i * SUB, SUB)
            s = lax.dot_general(kv_ref[k, part, 0:HD], q, across, preferred_element_type=F32)
            dp = lax.dot_general(
                kv_ref[k, part, HD:2 * HD], do, across, preferred_element_type=F32
            )
            p = jnp.exp2(s * (SCALE * LOG2E) - rows_ref[t, 0:1, :])
            if masked:
                index = (lax.broadcasted_iota(jnp.int32, (SUB, QT), 0) + i * SUB).astype(F32)
                p = jnp.where((index >= low) & (index < high), p, 0.0)
            p_ref[part, :] = p.astype(BF)
            ds_ref[part, :] = (p * (dp - rows_ref[t, 1:2, :])).astype(BF)

    def step(n, carry):
        whole = full_list[n + 1] == 1

        @pl.when(whole)
        def _():
            work(n, False)

        @pl.when(jnp.logical_not(whole))
        def _():
            work(n, True)

        return carry

    lax.fori_loop(0, count, step, 0)

    def emit(k, carry):
        dkv_ref[k, :, 0:HD] = (dk_acc[k] * SCALE).astype(BF)
        dkv_ref[k, :, HD:2 * HD] = dv_acc[k].astype(BF)
        for i in range(NQT // NKT):
            t = k * (NQT // NKT) + i
            dq = (dq_acc[t] * SCALE).T
            dq_ref[pl.ds(t * TILE_G, TILE_G)] = dq.astype(BF).reshape(TILE_G, ROWS, HD)
        return carry

    lax.fori_loop(0, NKT, emit, 0)


N_REDUCE = 16 + 16 + 7 + 7 + 4 + 1 + 2 + 2 + 7


def reduce_kernel(
    kv_ref, dq_in, gq_ref, gk_ref, gv_ref,
    far, near, out_x, ring_in, ring_out, both_in, both_out, both_sum, b_far, b_near, b_out,
    q_twin, q_sum, q_far, q_near, q_out, q_send, q_back, send, recv,
):
    z, y, x, c = place()
    xp, xm, xo = (x + 1) % NX, (x + 3) % NX, (x + 2) % NX
    yp, ym, yo = (y + 1) % NY, (y + 3) % NY, (y + 2) % NY
    zp, zm = (z + 1) % NZ, (z + NZ - 1) % NZ
    right, left = device(z, y, xp, c), device(z, y, xm, c)
    up, down = device(z, yp, x, c), device(z, ym, x, c)
    z_right, z_left = device(zp, y, x, c), device(zm, y, x, c)
    twin = device(z, y, x, 1 - c)
    planes = [(z + d) % NZ for d in range(1, NZ)]
    greet([right, left, up, down, twin] + [device(w, y, x, c) for w in planes])
    copies = Copies(send, recv)
    start = copies.start
    h = ROUND // 2
    rest = pl.ds(ROUND, BOTH)
    order = [4, 3, -3, 2, -2, 1, -1, 0]

    def first(n):
        zb = (z + NZ + order[n]) % NZ
        return (
            start(kv_ref.at[zb, xo, pl.ds(0, h)], far.at[n, 0], right),
            start(kv_ref.at[zb, xo, pl.ds(h, h)], far.at[n, 1], left),
        )

    def second(n, pair):
        zb = (z + NZ + order[n]) % NZ
        pair[0].wait_recv()
        out_x[n, 0, 0:h] = (kv_ref[zb, xp, 0:h].astype(F32) + far[n, 0].astype(F32)).astype(BF)
        out_x[n, 0, h:ROUND] = kv_ref[zb, xp, h:ROUND]
        a = start(out_x.at[n, 0], near.at[n, 0], right)
        pair[1].wait_recv()
        out_x[n, 1, 0:h] = kv_ref[zb, xm, 0:h]
        out_x[n, 1, h:ROUND] = (kv_ref[zb, xm, h:ROUND].astype(F32) + far[n, 1].astype(F32)).astype(BF)
        b = start(out_x.at[n, 1], near.at[n, 1], left)
        return a, b

    ring = {}

    def third(n, pair):
        off = order[n]
        zb = (z + NZ + off) % NZ
        pair[0].wait_recv()
        pair[1].wait_recv()
        total = kv_ref[zb, x, 0:ROUND].astype(F32) + near[n, 0].astype(F32) + near[n, 1].astype(F32)
        if off > 0:
            hop = 4 - off
            if hop > 0:
                ring[("r", hop)].wait_recv()
                total += ring_in[hop - 1].astype(F32)
            ring_out[n] = total.astype(BF)
            ring[("r", hop + 1)] = start(ring_out.at[n], ring_in.at[hop], z_right)
        elif off < 0:
            hop = 3 + off
            if hop > 0:
                ring[("l", hop)].wait_recv()
                total += ring_in[4 + hop - 1].astype(F32)
            ring_out[n] = total.astype(BF)
            ring[("l", hop + 1)] = start(ring_out.at[n], ring_in.at[4 + hop], z_left)
        else:
            ring[("r", 4)].wait_recv()
            ring[("l", 3)].wait_recv()
            total += ring_in[3].astype(F32) + ring_in[6].astype(F32)
            gk_ref[0:ROUND] = total[:, 0:HD].astype(BF)
            gv_ref[0:ROUND] = total[:, HD:2 * HD].astype(BF)

    def both(s):
        if s == 0:
            ring["R", 1] = start(kv_ref.at[(z + 3) % NZ, :, rest], both_in.at[0], z_right)
            ring["L", 1] = start(kv_ref.at[(z + 4) % NZ, :, rest], both_in.at[3], z_left)
            return
        if s < 4:
            ring["R", s].wait_recv()
        if s < 3:
            mine = kv_ref[(z + 3 - s) % NZ, :, ROUND:TOK].astype(F32)
            both_out[s - 1] = (mine + both_in[s - 1].astype(F32)).astype(BF)
            ring["R", s + 1] = start(both_out.at[s - 1], both_in.at[s], z_right)
        if s < 5:
            ring["L", s].wait_recv()
        if s < 4:
            mine = kv_ref[(z + 4 + s) % NZ, :, ROUND:TOK].astype(F32)
            both_out[1 + s] = (mine + both_in[2 + s].astype(F32)).astype(BF)
            ring["L", s + 1] = start(both_out.at[1 + s], both_in.at[3 + s], z_left)
        if s == 4:
            both_sum[...] = (
                kv_ref[z, :, ROUND:TOK].astype(F32)
                + both_in[2].astype(F32)
                + both_in[6].astype(F32)
            ).astype(BF)
            b = BOTH // 2
            ring["f", 0] = start(both_sum.at[xo, pl.ds(0, b)], b_far.at[0], right)
            ring["f", 1] = start(both_sum.at[xo, pl.ds(b, b)], b_far.at[1], left)
        if s == 5:
            b = BOTH // 2
            ring["f", 0].wait_recv()
            b_out[0, 0:b] = (both_sum[xp, 0:b].astype(F32) + b_far[0].astype(F32)).astype(BF)
            b_out[0, b:BOTH] = both_sum[xp, b:BOTH]
            ring["n", 0] = start(b_out.at[0], b_near.at[0], right)
            ring["f", 1].wait_recv()
            b_out[1, 0:b] = both_sum[xm, 0:b]
            b_out[1, b:BOTH] = (both_sum[xm, b:BOTH].astype(F32) + b_far[1].astype(F32)).astype(BF)
            ring["n", 1] = start(b_out.at[1], b_near.at[1], left)

    def both_end():
        ring["n", 0].wait_recv()
        ring["n", 1].wait_recv()
        total = both_sum[x].astype(F32) + b_near[0].astype(F32) + b_near[1].astype(F32)
        gk_ref[ROUND:TOK] = total[:, 0:HD].astype(BF)
        gv_ref[ROUND:TOK] = total[:, HD:2 * HD].astype(BF)

    queue = {}

    def q_step(s):
        if s == 0:
            queue["twin"] = start(dq_in.at[:, :, 1 - c], q_twin, twin)
        elif s == 1:
            queue["twin"].wait_recv()
            for zz in range(NZ):
                q_sum[zz] = (dq_in[zz, :, c].astype(F32) + q_twin[zz].astype(F32)).astype(BF)
            queue["a"] = start(q_sum.at[pl.ds(0, 4), yo // 2, yo % 2], q_far.at[0], up)
            queue["b"] = start(q_sum.at[pl.ds(4, 4), yo // 2, yo % 2], q_far.at[1], down)
        elif s == 2:
            queue["a"].wait_recv()
            q_out[0, 0:4] = (
                q_sum[0:4, yp // 2, yp % 2].astype(F32) + q_far[0].astype(F32)
            ).astype(BF)
            q_out[0, 4:8] = q_sum[4:8, yp // 2, yp % 2]
            queue["c"] = start(q_out.at[0], q_near.at[0], up)
            queue["b"].wait_recv()
            q_out[1, 0:4] = q_sum[0:4, ym // 2, ym % 2]
            q_out[1, 4:8] = (
                q_sum[4:8, ym // 2, ym % 2].astype(F32) + q_far[1].astype(F32)
            ).astype(BF)
            queue["d"] = start(q_out.at[1], q_near.at[1], down)
        else:
            queue["c"].wait_recv()
            queue["d"].wait_recv()
            q_send[...] = (
                q_sum[:, y // 2, y % 2].astype(F32)
                + q_near[0].astype(F32)
                + q_near[1].astype(F32)
            ).astype(BF)
            queue["back"] = [
                start(q_send.at[w], q_back.at[z], device(w, y, x, c)) for w in planes
            ]
            q_back[z] = q_send[z]

    one, two = {}, {}

    def x_far(n):
        one[n] = first(n)

    def x_near(n):
        two[n] = second(n, one[n])

    def x_sum(n):
        third(n, two[n])

    for do, which in [
        (q_step, 0), (x_far, 0), (both, 0), (x_far, 1), (x_far, 2), (x_far, 3), (x_near, 0),
        (x_far, 4), (x_near, 1), (x_far, 5), (both, 1), (q_step, 1), (x_sum, 0), (x_near, 2),
        (x_far, 6), (x_near, 3), (both, 2), (q_step, 2), (x_sum, 1), (x_near, 4), (x_far, 7),
        (x_sum, 2), (x_near, 5), (both, 3), (x_near, 6), (x_sum, 3), (x_sum, 4), (q_step, 3),
        (both, 4), (x_near, 7), (x_sum, 5), (x_sum, 6), (both, 5), (x_sum, 7),
    ]:
        do(which)
    both_end()
    for copy in queue["back"]:
        copy.wait_recv()
    for w in range(NZ):
        for head in range(GROUP):
            gq_ref[w * PIECE:(w + 1) * PIECE, head * HD:(head + 1) * HD] = q_back[
                w, head * PIECE:(head + 1) * PIECE
            ]
    assert copies.count == N_REDUCE, copies.count
    copies.finish()


def body(queries, keys, values, outputs, out_grad, log_sum_exp, segment_ids):
    hbm = pl.BlockSpec(memory_space=pltpu.HBM)
    vmem = pl.BlockSpec(memory_space=pltpu.VMEM)

    kv_all, qd_all, st_all, sg_all = pl.pallas_call(
        gather_kernel,
        out_shape=[
            jax.ShapeDtypeStruct((NZ, NX, TOK, 2 * HD), BF),
            jax.ShapeDtypeStruct((NZ, 2, NC, 2, 2, ROWS, HD), BF),
            jax.ShapeDtypeStruct((NZ, 2, NC, 2, 2, 128), F32),
            jax.ShapeDtypeStruct((NZ, NX, 1, TOK), F32),
        ],
        in_specs=[hbm] * 7,
        out_specs=[vmem] * 4,
        scratch_shapes=[
            pltpu.VMEM((TOK, GROUP * HD), BF),
            pltpu.VMEM((TOK, GROUP * HD), BF),
            pltpu.VMEM((TOK, GROUP * HD), BF),
            pltpu.VMEM((GROUP, TOK), F32),
            pltpu.VMEM((1, TOK), jnp.int32),
            pltpu.VMEM((NZ, 2, ROWS, HD), BF),
            pltpu.VMEM((NZ, 2, 2 * ROWS), F32),
            pltpu.SemaphoreType.DMA((N_GATHER,)),
            pltpu.SemaphoreType.DMA((N_GATHER,)),
            pltpu.SemaphoreType.DMA((7,)),
        ],
        compiler_params=pltpu.CompilerParams(
            collective_id=0, has_side_effects=True, vmem_limit_bytes=40 * 2**20
        ),
        name="gather",
    )(
        *[
            pltpu.with_memory_space_constraint(a, pltpu.HBM)
            for a in (
                queries, keys, values, outputs, out_grad,
                log_sum_exp.T, segment_ids.reshape(1, TOK),
            )
        ]
    )

    dkv, dq = pl.pallas_call(
        attend_kernel,
        out_shape=[
            jax.ShapeDtypeStruct((NKT, KT, 2 * HD), BF),
            jax.ShapeDtypeStruct((NG, ROWS, HD), BF),
        ],
        in_specs=[vmem] * 4,
        out_specs=[vmem] * 2,
        scratch_shapes=[
            pltpu.VMEM((NQT, 8, QT), F32),
            pltpu.VMEM((NQT, HD, QT), F32),
            pltpu.VMEM((NKT, KT, HD), F32),
            pltpu.VMEM((NKT, KT, HD), F32),
            pltpu.VMEM((NKT, HD, KT), BF),
            pltpu.VMEM((KT, QT), BF),
            pltpu.VMEM((KT, QT), BF),
            pltpu.SMEM((NQT,), jnp.int32),
            pltpu.SMEM((NQT,), jnp.int32),
            pltpu.SMEM((STEPS,), jnp.int32),
            pltpu.SMEM((STEPS,), jnp.int32),
            pltpu.SMEM((STEPS,), jnp.int32),
            pltpu.SMEM((STEPS,), jnp.int32),
        ],
        compiler_params=pltpu.CompilerParams(vmem_limit_bytes=40 * 2**20),
        name="attend",
    )(
        kv_all.reshape(NKT, KT, 2 * HD),
        qd_all.reshape(NG, 2, ROWS, HD),
        st_all.reshape(NG, 2, 128),
        sg_all.reshape(NZ * NX, 1, TOK),
    )

    return pl.pallas_call(
        reduce_kernel,
        out_shape=[
            jax.ShapeDtypeStruct((TOK, GROUP * HD), BF),
            jax.ShapeDtypeStruct((TOK, HD), BF),
            jax.ShapeDtypeStruct((TOK, HD), BF),
        ],
        in_specs=[vmem] * 2,
        out_specs=[vmem] * 3,
        scratch_shapes=[
            pltpu.VMEM((NZ, 2, ROUND // 2, 2 * HD), BF),
            pltpu.VMEM((NZ, 2, ROUND, 2 * HD), BF),
            pltpu.VMEM((NZ, 2, ROUND, 2 * HD), BF),
            pltpu.VMEM((7, ROUND, 2 * HD), BF),
            pltpu.VMEM((7, ROUND, 2 * HD), BF),
            pltpu.VMEM((7, NX, BOTH, 2 * HD), BF),
            pltpu.VMEM((5, NX, BOTH, 2 * HD), BF),
            pltpu.VMEM((NX, BOTH, 2 * HD), BF),
            pltpu.VMEM((2, BOTH // 2, 2 * HD), BF),
            pltpu.VMEM((2, BOTH, 2 * HD), BF),
            pltpu.VMEM((2, BOTH, 2 * HD), BF),
            pltpu.VMEM((NZ, 2, 2, ROWS, HD), BF),
            pltpu.VMEM((NZ, 2, 2, ROWS, HD), BF),
            pltpu.VMEM((2, 4, ROWS, HD), BF),
            pltpu.VMEM((2, NZ, ROWS, HD), BF),
            pltpu.VMEM((2, NZ, ROWS, HD), BF),
            pltpu.VMEM((NZ, ROWS, HD), BF),
            pltpu.VMEM((NZ, ROWS, HD), BF),
            pltpu.SemaphoreType.DMA((N_REDUCE,)),
            pltpu.SemaphoreType.DMA((N_REDUCE,)),
        ],
        compiler_params=pltpu.CompilerParams(
            collective_id=1, has_side_effects=True, vmem_limit_bytes=40 * 2**20
        ),
        name="reduce",
    )(
        dkv.reshape(NZ, NX, TOK, 2 * HD),
        dq.reshape(NZ, 2, NC, 2, ROWS, HD),
    )


def solution(mesh):
    rows = P(("row", "col"), None)
    return jax.shard_map(
        body,
        mesh=mesh,
        in_specs=(rows, rows, rows, rows, rows, rows, P(("row", "col"))),
        out_specs=(rows, rows, rows),
        check_vma=False,
    )
```

```python
import functools
import math

import jax
import jax.numpy as jnp
from jax import lax
from jax.experimental import pallas as pl
from jax.experimental.pallas import tpu as pltpu
from jax.sharding import PartitionSpec as P

MESH = pl.DeviceIdType.MESH
HD = 128
GROUP = 4
NZ, NY, NX, NC = 8, 4, 4, 2
TOK = 128
PIECE = TOK // NZ
ROWS = PIECE * GROUP
NG = NZ * NY * NC
TILE_G = 4
NQT = NG // TILE_G
QT = TILE_G * ROWS
KT = 512
SUB = 128
ROUND = 96
BOTH = TOK - ROUND
NKEY = NZ * NX * TOK
NKT = NKEY // KT
CHUNK = NX * TOK
IDS = 72
STEPS = NQT * NKT + 8
SCALE = HD ** -0.5
LOG2E = math.log2(math.e)
BF = jnp.bfloat16
F32 = jnp.float32


def place():
    row = lax.axis_index("row")
    col = lax.axis_index("col")
    z = row // 4
    y = (row // 2) % 2 * 2 + col // 4
    return z, y, col % 4, row % 2


def device(z, y, x, c):
    return (z * 4 + y // 2 * 2 + c, y % 2 * 4 + x)


def origin(z, y, x, c):
    return y // 2 * 2048 + c * 1024 + y % 2 * 512, x * TOK + z * PIECE, c * 2 + y % 2


def tile_start(t, shift):
    return jnp.minimum(t * TILE_G + shift, NG - TILE_G)


class Copies:
    def __init__(self, send, recv):
        self.send, self.recv, self.count, self.all = send, recv, 0, []

    def start(self, src, dst, to):
        i = self.count
        self.count += 1
        copy = pltpu.make_async_remote_copy(
            src_ref=src,
            dst_ref=dst,
            send_sem=self.send.at[i],
            recv_sem=self.recv.at[i],
            device_id=to,
            device_id_type=MESH,
        )
        copy.start()
        self.all.append(copy)
        return copy

    def finish(self):
        for copy in self.all:
            copy.wait_send()


def greet(peers, meanwhile=None):
    barrier = pltpu.get_barrier_semaphore()
    for peer in peers:
        pl.semaphore_signal(barrier, inc=1, device_id=peer, device_id_type=MESH)
    if meanwhile is not None:
        meanwhile()
    pl.semaphore_wait(barrier, len(peers))


N_GATHER = 32 + 7 + 7 + 24 + 4 + 11 + 10


def gather_kernel(
    q_in, k_in, v_in, o_in, do_in, lse_in, seg_in, kv_all, qd_all, keys_t, rows_ref,
    st_all, sg_all, q_ref, o_ref, do_ref, lse_ref, seg_ref, qd_ref, st_ref, send, recv, local,
):
    z, y, x, c = place()
    xp, xm, xo = (x + 1) % NX, (x + 3) % NX, (x + 2) % NX
    yp, ym, yo = (y + 1) % NY, (y + 3) % NY, (y + 2) % NY
    zp, zm = (z + 1) % NZ, (z + NZ - 1) % NZ
    right, left, across = device(z, y, xp, c), device(z, y, xm, c), device(z, y, xo, c)
    up, down, beyond = device(z, yp, x, c), device(z, ym, x, c), device(z, yo, x, c)
    z_right, z_left = device(zp, y, x, c), device(zm, y, x, c)
    twin = device(z, y, x, 1 - c)
    planes = [(z + d) % NZ for d in range(1, NZ)]
    load = [
        pltpu.make_async_copy(src, dst, local.at[i])
        for i, (src, dst) in enumerate([
            (k_in, kv_all.at[z, x, :, pl.ds(0, HD)]),
            (v_in, kv_all.at[z, x, :, pl.ds(HD, HD)]),
            (q_in, q_ref),
            (do_in, do_ref),
            (o_in, o_ref),
            (lse_in, lse_ref),
            (seg_in, seg_ref),
        ])
    ]
    for copy in load:
        copy.start()
    greet(
        [right, left, across, up, down, beyond, twin] + [device(w, y, x, c) for w in planes]
    )
    copies = Copies(send, recv)
    start = copies.start
    yh, yl = y // 2, y % 2

    near, far, hops, pieces, q_near, q_far = {}, {}, {}, {}, {}, []
    few, ends = {}, []
    steps = [0, 1, -1, 2, -2, 3, -3, 4]
    h = TOK // 2

    def ring(s):
        if 0 < s < 4:
            hops["r", s].wait_recv()
        if s < 3:
            src = kv_all.at[(z + NZ - s) % NZ, x]
            hops["r", s + 1] = start(src, src, z_right)
        if s > 0:
            hops["l", s].wait_recv()
        if s < 4:
            src = kv_all.at[(z + s) % NZ, x]
            hops["l", s + 1] = start(src, src, z_left)

    def spread(d):
        src = kv_all.at[(z + NZ + d) % NZ, x]
        near[d] = (start(src, src, right), start(src, src, left))

    def pass_on(d):
        zb = (z + NZ + d) % NZ
        near[d][0].wait_recv()
        src = kv_all.at[zb, xm, pl.ds(0, h)]
        far[d] = [start(src, src, right)]
        near[d][1].wait_recv()
        src = kv_all.at[zb, xp, pl.ds(h, h)]
        far[d].append(start(src, src, left))

    def pack(_):
        load[2].wait()
        load[3].wait()
        for w in range(NZ):
            for g in range(GROUP):
                here = (slice(w * PIECE, (w + 1) * PIECE), slice(g * HD, (g + 1) * HD))
                there = slice(g * PIECE, (g + 1) * PIECE)
                qd_ref[w, 0, there] = q_ref[here]
                qd_ref[w, 1, there] = do_ref[here]
        qd_all[z, yh, c, yl] = qd_ref[z]

    def q_send(d):
        w = (z + NZ + d) % NZ
        pieces[d] = start(qd_ref.at[w], qd_all.at[z, yh, c, yl], device(w, y, x, c))

    def q_share(d):
        if d != 0:
            pieces[d].wait_recv()
        src = qd_all.at[(z + NZ - d) % NZ, yh, c, yl]
        q_near[d] = (start(src, src, up), start(src, src, down))

    def q_pass(d):
        zz = (z + NZ - d) % NZ
        q_near[d][0].wait_recv()
        q_near[d][1].wait_recv()
        if steps.index(d) % 2 == 0:
            src = qd_all.at[zz, ym // 2, c, ym % 2]
            q_far.append(start(src, src, up))
        else:
            src = qd_all.at[zz, yp // 2, c, yp % 2]
            q_far.append(start(src, src, down))

    def q_across(where):
        if where == 2:
            for copy in q_far:
                copy.wait_recv()
        for yy in ((y,), (yp, ym), (yo,))[where]:
            src = qd_all.at[:, yy // 2, c, yy % 2]
            ends.append(start(src, src, twin))

    def stats(stage):
        if stage == 0:
            for copy in load[4:]:
                copy.wait()
            sub = lax.broadcasted_iota(jnp.int32, (TOK, TOK), 0)
            lane = lax.broadcasted_iota(jnp.int32, (TOK, TOK), 1)
            dots = []
            for g in range(GROUP):
                cols = slice(g * HD, (g + 1) * HD)
                both = lax.dot_general(
                    do_ref[:, cols], o_ref[:, cols], (((1,), (1,)), ((), ())),
                    preferred_element_type=F32,
                )
                dots.append(jnp.sum(jnp.where(sub == lane, both, 0.0), axis=0, keepdims=True))
            numbers = jnp.concatenate([lse_ref[...]] + dots, axis=0)
            seg = seg_ref[...].astype(F32)
            sg_all[z, x] = seg
            segs = jnp.broadcast_to(seg, (2 * GROUP, TOK))
            sub, block = sub[0:8], lane[0:8] // PIECE
            turned = [
                [a if d == 0 else pltpu.roll(a, d * PIECE, 1) for d in range(NZ)]
                for a in (numbers, segs)
            ]
            for w in range(NZ):
                for i in range(2):
                    row = jnp.zeros((8, TOK), F32)
                    for d in range(NZ):
                        fits = (block == sub) & ((sub + NZ - w) % NZ == d)
                        row += jnp.where(fits, turned[i][d], 0.0)
                    st_ref[w, i:i + 1, :] = jnp.sum(row, axis=0, keepdims=True)
            st_all[z, yh, c, yl] = st_ref[z]
            few[0] = [
                start(st_ref.at[w], st_all.at[z, yh, c, yl], device(w, y, x, c)) for w in planes
            ]
            src = sg_all.at[z, x]
            few[0] += [start(src, src, device(w, y, x, c)) for w in planes]
        elif stage == 1:
            for copy in few[0]:
                copy.wait_recv()
            src = st_all.at[:, yh, c, yl]
            few[1] = [start(src, src, to) for to in (up, down, beyond)]
            src = sg_all.at[:, x]
            few[2] = [start(src, src, to) for to in (right, left, across)]
        else:
            for copy in few[1]:
                copy.wait_recv()
            src = st_all.at[:, :, c]
            few[2].append(start(src, src, twin))

    def turn(d):
        zb = (z + NZ + d) % NZ
        for copy in far[d]:
            copy.wait_recv()
        for i in range(NX):
            keys_t[zb, :, i * TOK:(i + 1) * TOK] = kv_all[zb, i, :, 0:HD].T

    def ranges(_):
        for copy in few[2]:
            copy.wait_recv()
        key_start, query_start, shift = origin(z, y, x, c)
        ids = lax.broadcasted_iota(jnp.int32, (IDS, TOK), 0).astype(F32)
        before = jnp.zeros((IDS, TOK), F32)
        for zz in range(NZ):
            for xx in range(NX):
                before += jnp.where(sg_all[zz, xx] < ids, 1.0, 0.0)
        before = jnp.sum(before, axis=1, keepdims=True)
        id_col = lax.broadcasted_iota(jnp.int32, (IDS, QT), 0).astype(F32)
        half = lax.broadcasted_iota(jnp.int32, (1, 128), 1) < ROWS
        lane = lax.broadcasted_iota(jnp.int32, (1, QT), 1)

        def one_tile(t, carry):
            first = t * TILE_G + shift
            g = tile_start(t, shift)

            def numbers(i, row):
                p = g + i
                return st_all[p // 8, p // 4 % 2, p // 2 % 2, p % 2, row:row + 1, :]

            def pair(a, b):
                return jnp.where(half, a, b)

            own = [numbers(i, 0) for i in range(TILE_G)]
            over = [pltpu.roll(a, ROWS, 1) for a in own]
            lse = jnp.concatenate([pair(own[0], over[1]), pair(own[2], over[3])], axis=1)
            dot = jnp.concatenate([pair(over[0], own[1]), pair(over[2], own[3])], axis=1)
            seg = [numbers(i, 1) for i in range(TILE_G)]
            seg = jnp.concatenate([pair(seg[0], seg[1]), pair(seg[2], seg[3])], axis=1)
            lo = jnp.sum(jnp.where(id_col == seg, before, 0.0), axis=0, keepdims=True)
            piece = g + lane // ROWS
            rem = piece % NZ * CHUNK + query_start + lane % PIECE - key_start
            hi = piece // NZ * CHUNK + jnp.clip(rem + 1, 0, CHUNK)
            fresh = piece >= first
            rows_ref[t, 0:1, :] = lse * LOG2E
            rows_ref[t, 1:2, :] = dot
            rows_ref[t, 2:3, :] = jnp.where(fresh, lo, float(NKEY))
            rows_ref[t, 3:4, :] = jnp.where(fresh, hi, 0).astype(F32)
            return carry

        lax.fori_loop(0, NQT, one_tile, 0)

    load[0].wait()
    load[1].wait()
    for do, which in [
        (spread, 0), (ring, 0), (pack, 0), (q_send, -1), (q_share, 0), (q_send, 3), (q_send, -2),
        (ring, 1), (q_send, -3), (q_send, 1), (spread, 1), (q_send, 4), (pass_on, 0),
        (spread, -1), (stats, 0), (q_share, 3), (q_share, -1), (ring, 2), (spread, -2),
        (q_send, 2), (spread, 2), (q_pass, 3), (pass_on, -1), (q_share, -2), (stats, 1),
        (q_pass, 0), (pass_on, -2), (q_share, 4), (pass_on, 1), (ring, 3), (q_share, 1),
        (spread, -3), (q_share, -3), (spread, 3), (q_share, 2), (q_pass, -2), (stats, 2),
        (turn, -2), (turn, -1), (q_pass, 1), (q_pass, 4), (q_across, 0), (q_pass, -1), (ring, 4),
        (spread, 4), (pass_on, 2), (pass_on, -3), (q_pass, -3), (q_pass, 2), (q_across, 1),
        (ranges, 0), (turn, 1), (pass_on, 3), (pass_on, 4), (q_across, 2), (turn, 2), (turn, 0),
        (turn, 3), (turn, -3), (turn, 4),
    ]:
        do(which)
    for copy in ends:
        copy.wait_recv()
    assert copies.count == N_GATHER, copies.count
    copies.finish()


def attend_kernel(
    kv_ref, qd_ref, keys_t, rows_ref, dq_acc, dk_acc, dv_acc, p_ref, ds_ref,
    low_ref, k_list, t_list, from_list,
):
    z, y, x, c = place()
    shift = origin(z, y, x, c)[2]

    def piece(t):
        return tile_start(t, shift)

    for t in range(NQT):
        low_ref[t] = jnp.min(rows_ref[t, 2:3, :]).astype(jnp.int32)

    def clear(k, carry):
        dq_acc[2 * k] = jnp.zeros((HD, QT), F32)
        dq_acc[2 * k + 1] = jnp.zeros((HD, QT), F32)
        dk_acc[k] = jnp.zeros((KT, HD), F32)
        dv_acc[k] = jnp.zeros((KT, HD), F32)
        return carry

    lax.fori_loop(0, NKT, clear, 0)
    p_ref[...] = jnp.zeros((2, KT, QT), BF)
    ds_ref[...] = jnp.zeros((2, KT, QT), BF)

    def nothing(n):
        k_list[n] = 0
        t_list[n] = 0
        from_list[n] = -(1 << 20)

    nothing(0)
    nothing(1)
    lows = [low_ref[t] for t in range(NQT)]

    def listed(k, count):
        end = 0
        for low in lows:
            end += jnp.where(low < (k + 1) * KT, 1, 0)

        def note(t, count):
            k_list[count] = k
            t_list[count] = t
            from_list[count] = k * KT
            return count + 1

        return lax.fori_loop(2 * k + y // 2, end, note, count)

    count = lax.fori_loop(0, NKT, listed, 2)
    for i in range(3):
        nothing(count + i)

    def sums(n, slot):
        k, t = k_list[n], t_list[n]
        q = qd_ref[pl.ds(piece(t), TILE_G), 0].reshape(QT, HD)
        do = qd_ref[pl.ds(piece(t), TILE_G), 1].reshape(QT, HD)
        p, ds = p_ref[slot], ds_ref[slot]
        dv_acc[k] += jnp.dot(p, do, preferred_element_type=F32)
        dk_acc[k] += jnp.dot(ds, q, preferred_element_type=F32)
        dq_acc[t] += jnp.dot(keys_t[k], ds, preferred_element_type=F32)

    def probabilities(n, slot):
        k, t = k_list[n], t_list[n]
        q = qd_ref[pl.ds(piece(t), TILE_G), 0].reshape(QT, HD)
        do = qd_ref[pl.ds(piece(t), TILE_G), 1].reshape(QT, HD)
        start = from_list[n].astype(F32)
        low = rows_ref[t, 2:3, :] - start
        high = rows_ref[t, 3:4, :] - start
        across = (((1,), (1,)), ((), ()))
        for i in range(KT // SUB):
            part = pl.ds(i * SUB, SUB)
            s = lax.dot_general(kv_ref[k, part, 0:HD], q, across, preferred_element_type=F32)
            dp = lax.dot_general(
                kv_ref[k, part, HD:2 * HD], do, across, preferred_element_type=F32
            )
            index = (lax.broadcasted_iota(jnp.int32, (SUB, QT), 0) + i * SUB).astype(F32)
            p = jnp.exp2(s * (SCALE * LOG2E) - rows_ref[t, 0:1, :])
            p = jnp.where((index >= low) & (index < high), p, 0.0)
            p_ref[slot, part, :] = p.astype(BF)
            ds_ref[slot, part, :] = (p * (dp - rows_ref[t, 1:2, :])).astype(BF)

    def step(i, carry):
        n = 2 * i
        sums(n, 0)
        sums(n + 1, 1)
        probabilities(n + 2, 0)
        probabilities(n + 3, 1)
        return carry

    lax.fori_loop(0, (count + 1) // 2, step, 0)


N_REDUCE = 16 + 16 + 7 + 7 + 4 + 1 + 2 + 2 + 7


def reduce_kernel(
    dq_acc, dk_acc, dv_acc, gq_ref, gk_ref, gv_ref, kv_ref, dq_in,
    far, near, out_x, ring_in, ring_out, both_in, both_out, both_sum, b_far, b_near, b_out,
    q_twin, q_sum, q_far, q_near, q_out, q_send, q_back, send, recv,
):
    z, y, x, c = place()
    xp, xm, xo = (x + 1) % NX, (x + 3) % NX, (x + 2) % NX
    yp, ym, yo = (y + 1) % NY, (y + 3) % NY, (y + 2) % NY
    zp, zm = (z + 1) % NZ, (z + NZ - 1) % NZ
    right, left = device(z, y, xp, c), device(z, y, xm, c)
    up, down = device(z, yp, x, c), device(z, ym, x, c)
    z_right, z_left = device(zp, y, x, c), device(zm, y, x, c)
    twin = device(z, y, x, 1 - c)
    planes = [(z + d) % NZ for d in range(1, NZ)]
    shift = origin(z, y, x, c)[2]

    def rounded():
        def keys_side(k, carry):
            for i in range(NX):
                part = pl.ds(i * TOK, TOK)
                kv_ref[k, i, :, 0:HD] = (dk_acc[k, part] * SCALE).astype(BF)
                kv_ref[k, i, :, HD:2 * HD] = dv_acc[k, part].astype(BF)
            return carry

        def queries_side(i, carry):
            for j in range(2):
                t = NQT - 1 - 2 * i - j
                dq = (dq_acc[t] * SCALE).astype(BF).T.reshape(TILE_G, ROWS, HD)
                for e in range(TILE_G):
                    g = tile_start(t, shift) + e
                    dq_in[g // 8, g // 4 % 2, g // 2 % 2, g % 2] = dq[e]
            return carry

        for g in range(TILE_G):
            dq_in[0, 0, g // 2, g % 2] = jnp.zeros((ROWS, HD), BF)
        lax.fori_loop(0, NQT // 2, queries_side, 0)
        lax.fori_loop(0, NKT, keys_side, 0)

    greet([right, left, up, down, twin] + [device(w, y, x, c) for w in planes], rounded)
    copies = Copies(send, recv)
    start = copies.start
    h = ROUND // 2
    rest = pl.ds(ROUND, BOTH)
    order = [4, 3, -3, 2, -2, 1, -1, 0]

    def first(n):
        zb = (z + NZ + order[n]) % NZ
        return (
            start(kv_ref.at[zb, xo, pl.ds(0, h)], far.at[n, 0], right),
            start(kv_ref.at[zb, xo, pl.ds(h, h)], far.at[n, 1], left),
        )

    def second(n, pair):
        zb = (z + NZ + order[n]) % NZ
        pair[0].wait_recv()
        out_x[n, 0, 0:h] = (kv_ref[zb, xp, 0:h].astype(F32) + far[n, 0].astype(F32)).astype(BF)
        out_x[n, 0, h:ROUND] = kv_ref[zb, xp, h:ROUND]
        a = start(out_x.at[n, 0], near.at[n, 0], right)
        pair[1].wait_recv()
        out_x[n, 1, 0:h] = kv_ref[zb, xm, 0:h]
        out_x[n, 1, h:ROUND] = (kv_ref[zb, xm, h:ROUND].astype(F32) + far[n, 1].astype(F32)).astype(BF)
        b = start(out_x.at[n, 1], near.at[n, 1], left)
        return a, b

    ring = {}

    def third(n, pair):
        off = order[n]
        zb = (z + NZ + off) % NZ
        pair[0].wait_recv()
        pair[1].wait_recv()
        total = kv_ref[zb, x, 0:ROUND].astype(F32) + near[n, 0].astype(F32) + near[n, 1].astype(F32)
        if off > 0:
            hop = 4 - off
            if hop > 0:
                ring[("r", hop)].wait_recv()
                total += ring_in[hop - 1].astype(F32)
            ring_out[n] = total.astype(BF)
            ring[("r", hop + 1)] = start(ring_out.at[n], ring_in.at[hop], z_right)
        elif off < 0:
            hop = 3 + off
            if hop > 0:
                ring[("l", hop)].wait_recv()
                total += ring_in[4 + hop - 1].astype(F32)
            ring_out[n] = total.astype(BF)
            ring[("l", hop + 1)] = start(ring_out.at[n], ring_in.at[4 + hop], z_left)
        else:
            ring[("r", 4)].wait_recv()
            ring[("l", 3)].wait_recv()
            total += ring_in[3].astype(F32) + ring_in[6].astype(F32)
            gk_ref[0:ROUND] = total[:, 0:HD].astype(BF)
            gv_ref[0:ROUND] = total[:, HD:2 * HD].astype(BF)

    def both(s):
        if s == 0:
            ring["R", 1] = start(kv_ref.at[(z + 3) % NZ, :, rest], both_in.at[0], z_right)
            ring["L", 1] = start(kv_ref.at[(z + 4) % NZ, :, rest], both_in.at[3], z_left)
            return
        if s < 4:
            ring["R", s].wait_recv()
        if s < 3:
            mine = kv_ref[(z + 3 - s) % NZ, :, ROUND:TOK].astype(F32)
            both_out[s - 1] = (mine + both_in[s - 1].astype(F32)).astype(BF)
            ring["R", s + 1] = start(both_out.at[s - 1], both_in.at[s], z_right)
        if s < 5:
            ring["L", s].wait_recv()
        if s < 4:
            mine = kv_ref[(z + 4 + s) % NZ, :, ROUND:TOK].astype(F32)
            both_out[1 + s] = (mine + both_in[2 + s].astype(F32)).astype(BF)
            ring["L", s + 1] = start(both_out.at[1 + s], both_in.at[3 + s], z_left)
        if s == 4:
            both_sum[...] = (
                kv_ref[z, :, ROUND:TOK].astype(F32)
                + both_in[2].astype(F32)
                + both_in[6].astype(F32)
            ).astype(BF)
            b = BOTH // 2
            ring["f", 0] = start(both_sum.at[xo, pl.ds(0, b)], b_far.at[0], right)
            ring["f", 1] = start(both_sum.at[xo, pl.ds(b, b)], b_far.at[1], left)
        if s == 5:
            b = BOTH // 2
            ring["f", 0].wait_recv()
            b_out[0, 0:b] = (both_sum[xp, 0:b].astype(F32) + b_far[0].astype(F32)).astype(BF)
            b_out[0, b:BOTH] = both_sum[xp, b:BOTH]
            ring["n", 0] = start(b_out.at[0], b_near.at[0], right)
            ring["f", 1].wait_recv()
            b_out[1, 0:b] = both_sum[xm, 0:b]
            b_out[1, b:BOTH] = (both_sum[xm, b:BOTH].astype(F32) + b_far[1].astype(F32)).astype(BF)
            ring["n", 1] = start(b_out.at[1], b_near.at[1], left)

    def both_end():
        ring["n", 0].wait_recv()
        ring["n", 1].wait_recv()
        total = both_sum[x].astype(F32) + b_near[0].astype(F32) + b_near[1].astype(F32)
        gk_ref[ROUND:TOK] = total[:, 0:HD].astype(BF)
        gv_ref[ROUND:TOK] = total[:, HD:2 * HD].astype(BF)

    queue = {}

    def q_step(s):
        if s == 0:
            queue["twin"] = start(dq_in.at[:, :, 1 - c], q_twin, twin)
        elif s == 1:
            queue["twin"].wait_recv()
            for zz in range(NZ):
                q_sum[zz] = (dq_in[zz, :, c].astype(F32) + q_twin[zz].astype(F32)).astype(BF)
            queue["a"] = start(q_sum.at[pl.ds(0, 4), yo // 2, yo % 2], q_far.at[0], up)
            queue["b"] = start(q_sum.at[pl.ds(4, 4), yo // 2, yo % 2], q_far.at[1], down)
        elif s == 2:
            queue["a"].wait_recv()
            q_out[0, 0:4] = (
                q_sum[0:4, yp // 2, yp % 2].astype(F32) + q_far[0].astype(F32)
            ).astype(BF)
            q_out[0, 4:8] = q_sum[4:8, yp // 2, yp % 2]
            queue["c"] = start(q_out.at[0], q_near.at[0], up)
            queue["b"].wait_recv()
            q_out[1, 0:4] = q_sum[0:4, ym // 2, ym % 2]
            q_out[1, 4:8] = (
                q_sum[4:8, ym // 2, ym % 2].astype(F32) + q_far[1].astype(F32)
            ).astype(BF)
            queue["d"] = start(q_out.at[1], q_near.at[1], down)
        else:
            queue["c"].wait_recv()
            queue["d"].wait_recv()
            q_send[...] = (
                q_sum[:, y // 2, y % 2].astype(F32)
                + q_near[0].astype(F32)
                + q_near[1].astype(F32)
            ).astype(BF)
            queue["back"] = [
                start(q_send.at[w], q_back.at[z], device(w, y, x, c)) for w in planes
            ]
            q_back[z] = q_send[z]

    one, two = {}, {}

    def x_far(n):
        one[n] = first(n)

    def x_near(n):
        two[n] = second(n, one[n])

    def x_sum(n):
        third(n, two[n])

    for do, which in [
        (q_step, 0), (x_far, 0), (both, 0), (x_far, 1), (x_far, 2), (x_far, 3), (x_near, 0),
        (x_far, 4), (x_far, 5), (both, 1), (q_step, 1), (x_near, 1), (x_near, 2), (x_sum, 0),
        (x_far, 6), (x_near, 3), (x_near, 4), (x_far, 7), (both, 2), (q_step, 2), (x_near, 5),
        (x_sum, 1), (x_sum, 2), (x_near, 6), (both, 3), (x_sum, 3), (x_sum, 4), (q_step, 3),
        (both, 4), (x_sum, 5), (x_near, 7), (x_sum, 6), (both, 5), (x_sum, 7),
    ]:
        do(which)
    both_end()
    for copy in queue["back"]:
        copy.wait_recv()
    for w in range(NZ):
        for g in range(GROUP):
            rows = slice(w * PIECE, (w + 1) * PIECE)
            gq_ref[rows, g * HD:(g + 1) * HD] = q_back[w, g * PIECE:(g + 1) * PIECE]
    assert copies.count == N_REDUCE, copies.count
    copies.finish()


def body(queries, keys, values, outputs, out_grad, log_sum_exp, segment_ids):
    hbm = pl.BlockSpec(memory_space=pltpu.HBM)
    vmem = pl.BlockSpec(memory_space=pltpu.VMEM)

    kv_all, qd_all, keys_t, row_data = pl.pallas_call(
        gather_kernel,
        out_shape=[
            jax.ShapeDtypeStruct((NZ, NX, TOK, 2 * HD), BF),
            jax.ShapeDtypeStruct((NZ, 2, NC, 2, 2, ROWS, HD), BF),
            jax.ShapeDtypeStruct((NKT, HD, KT), BF),
            jax.ShapeDtypeStruct((NQT, 8, QT), F32),
        ],
        in_specs=[hbm] * 7,
        out_specs=[vmem] * 4,
        scratch_shapes=[
            pltpu.VMEM((NZ, 2, NC, 2, 2, 128), F32),
            pltpu.VMEM((NZ, NX, 1, TOK), F32),
            pltpu.VMEM((TOK, GROUP * HD), BF),
            pltpu.VMEM((TOK, GROUP * HD), BF),
            pltpu.VMEM((TOK, GROUP * HD), BF),
            pltpu.VMEM((GROUP, TOK), F32),
            pltpu.VMEM((1, TOK), jnp.int32),
            pltpu.VMEM((NZ, 2, ROWS, HD), BF),
            pltpu.VMEM((NZ, 2, 2 * ROWS), F32),
            pltpu.SemaphoreType.DMA((N_GATHER,)),
            pltpu.SemaphoreType.DMA((N_GATHER,)),
            pltpu.SemaphoreType.DMA((7,)),
        ],
        compiler_params=pltpu.CompilerParams(
            collective_id=0, has_side_effects=True, vmem_limit_bytes=40 * 2**20
        ),
        name="gather",
    )(
        *[
            pltpu.with_memory_space_constraint(a, pltpu.HBM)
            for a in (
                queries, keys, values, outputs, out_grad,
                log_sum_exp.T, segment_ids.reshape(1, TOK),
            )
        ]
    )

    sums = pl.pallas_call(
        attend_kernel,
        out_shape=[
            jax.ShapeDtypeStruct((NQT, HD, QT), F32),
            jax.ShapeDtypeStruct((NKT, KT, HD), F32),
            jax.ShapeDtypeStruct((NKT, KT, HD), F32),
        ],
        in_specs=[vmem] * 4,
        out_specs=[vmem] * 3,
        scratch_shapes=[
            pltpu.VMEM((2, KT, QT), BF),
            pltpu.VMEM((2, KT, QT), BF),
            pltpu.SMEM((NQT,), jnp.int32),
            pltpu.SMEM((STEPS,), jnp.int32),
            pltpu.SMEM((STEPS,), jnp.int32),
            pltpu.SMEM((STEPS,), jnp.int32),
        ],
        compiler_params=pltpu.CompilerParams(vmem_limit_bytes=40 * 2**20),
        name="attend",
    )(
        kv_all.reshape(NKT, KT, 2 * HD),
        qd_all.reshape(NG, 2, ROWS, HD),
        keys_t,
        row_data,
    )

    return pl.pallas_call(
        reduce_kernel,
        out_shape=[
            jax.ShapeDtypeStruct((TOK, GROUP * HD), BF),
            jax.ShapeDtypeStruct((TOK, HD), BF),
            jax.ShapeDtypeStruct((TOK, HD), BF),
        ],
        in_specs=[vmem] * 3,
        out_specs=[vmem] * 3,
        scratch_shapes=[
            pltpu.VMEM((NZ, NX, TOK, 2 * HD), BF),
            pltpu.VMEM((NZ, 2, NC, 2, ROWS, HD), BF),
            pltpu.VMEM((NZ, 2, ROUND // 2, 2 * HD), BF),
            pltpu.VMEM((NZ, 2, ROUND, 2 * HD), BF),
            pltpu.VMEM((NZ, 2, ROUND, 2 * HD), BF),
            pltpu.VMEM((7, ROUND, 2 * HD), BF),
            pltpu.VMEM((7, ROUND, 2 * HD), BF),
            pltpu.VMEM((7, NX, BOTH, 2 * HD), BF),
            pltpu.VMEM((5, NX, BOTH, 2 * HD), BF),
            pltpu.VMEM((NX, BOTH, 2 * HD), BF),
            pltpu.VMEM((2, BOTH // 2, 2 * HD), BF),
            pltpu.VMEM((2, BOTH, 2 * HD), BF),
            pltpu.VMEM((2, BOTH, 2 * HD), BF),
            pltpu.VMEM((NZ, 2, 2, ROWS, HD), BF),
            pltpu.VMEM((NZ, 2, 2, ROWS, HD), BF),
            pltpu.VMEM((2, 4, ROWS, HD), BF),
            pltpu.VMEM((2, NZ, ROWS, HD), BF),
            pltpu.VMEM((2, NZ, ROWS, HD), BF),
            pltpu.VMEM((NZ, ROWS, HD), BF),
            pltpu.VMEM((NZ, ROWS, HD), BF),
            pltpu.SemaphoreType.DMA((N_REDUCE,)),
            pltpu.SemaphoreType.DMA((N_REDUCE,)),
        ],
        compiler_params=pltpu.CompilerParams(
            collective_id=1, has_side_effects=True, vmem_limit_bytes=40 * 2**20
        ),
        name="reduce",
    )(*sums)


def solution(mesh):
    rows = P(("row", "col"), None)
    return jax.shard_map(
        body,
        mesh=mesh,
        in_specs=(rows, rows, rows, rows, rows, rows, P(("row", "col"))),
        out_specs=(rows, rows, rows),
        check_vma=False,
    )
```

```python
import functools
import math

import jax
import jax.numpy as jnp
from jax import lax
from jax.experimental import pallas as pl
from jax.experimental.pallas import tpu as pltpu
from jax.sharding import PartitionSpec as P

MESH = pl.DeviceIdType.MESH
HD = 128
GROUP = 4
NZ, NY, NX, NC = 8, 4, 4, 2
TOK = 128
PIECE = TOK // NZ
ROWS = PIECE * GROUP
NG = NZ * NY * NC
TILE_G = 4
NQT = NG // TILE_G
QT = TILE_G * ROWS
KT = 512
SUB = 128
ROUND = 96
BOTH = TOK - ROUND
NKEY = NZ * NX * TOK
NKT = NKEY // KT
CHUNK = NX * TOK
IDS = 72
STEPS = NQT * NKT + 8
SCALE = HD ** -0.5
LOG2E = math.log2(math.e)
BF = jnp.bfloat16
F32 = jnp.float32


def place():
    row = lax.axis_index("row")
    col = lax.axis_index("col")
    z = row // 4
    y = (row // 2) % 2 * 2 + col // 4
    return z, y, col % 4, row % 2


def device(z, y, x, c):
    return (z * 4 + y // 2 * 2 + c, y % 2 * 4 + x)


def origin(z, y, x, c):
    return y // 2 * 2048 + c * 1024 + y % 2 * 512, x * TOK + z * PIECE, c * 2 + y % 2


def tile_start(t, shift):
    return jnp.minimum(t * TILE_G + shift, NG - TILE_G)


class Copies:
    def __init__(self, send, recv):
        self.send, self.recv, self.count, self.all = send, recv, 0, []

    def start(self, src, dst, to):
        i = self.count
        self.count += 1
        copy = pltpu.make_async_remote_copy(
            src_ref=src,
            dst_ref=dst,
            send_sem=self.send.at[i],
            recv_sem=self.recv.at[i],
            device_id=to,
            device_id_type=MESH,
        )
        copy.start()
        self.all.append(copy)
        return copy

    def finish(self):
        for copy in self.all:
            copy.wait_send()


def greet(peers, meanwhile=None):
    barrier = pltpu.get_barrier_semaphore()
    for peer in peers:
        pl.semaphore_signal(barrier, inc=1, device_id=peer, device_id_type=MESH)
    if meanwhile is not None:
        meanwhile()
    pl.semaphore_wait(barrier, len(peers))


N_GATHER = 34 + 9 + 7 + 24 + 4 + 11 + 10


def gather_kernel(
    q_in, k_in, v_in, o_in, do_in, lse_in, seg_in, kv_all, qd_all, keys_t, rows_ref,
    st_all, sg_all, q_ref, o_ref, do_ref, lse_ref, seg_ref, qd_ref, st_ref, send, recv, local,
):
    z, y, x, c = place()
    xp, xm, xo = (x + 1) % NX, (x + 3) % NX, (x + 2) % NX
    yp, ym, yo = (y + 1) % NY, (y + 3) % NY, (y + 2) % NY
    zp, zm = (z + 1) % NZ, (z + NZ - 1) % NZ
    right, left, across = device(z, y, xp, c), device(z, y, xm, c), device(z, y, xo, c)
    up, down, beyond = device(z, yp, x, c), device(z, ym, x, c), device(z, yo, x, c)
    z_right, z_left = device(zp, y, x, c), device(zm, y, x, c)
    twin = device(z, y, x, 1 - c)
    planes = [(z + d) % NZ for d in range(1, NZ)]
    load = [
        pltpu.make_async_copy(src, dst, local.at[i])
        for i, (src, dst) in enumerate([
            (k_in, kv_all.at[z, x, :, pl.ds(0, HD)]),
            (v_in, kv_all.at[z, x, :, pl.ds(HD, HD)]),
            (q_in, q_ref),
            (do_in, do_ref),
            (o_in, o_ref),
            (lse_in, lse_ref),
            (seg_in, seg_ref),
        ])
    ]
    for copy in load:
        copy.start()
    greet(
        [right, left, across, up, down, beyond, twin] + [device(w, y, x, c) for w in planes]
    )
    copies = Copies(send, recv)
    start = copies.start
    yh, yl = y // 2, y % 2

    near, far, hops, pieces, q_near, q_far = {}, {}, {}, {}, {}, []
    few, ends = {}, []
    steps = [0, 1, -1, 2, -2, 3, -3, 4]
    h = TOK // 2

    def block_to(d, to):
        if d != 0:
            src = kv_all.at[(z + NZ + d) % NZ, x]
            return [start(src, src, to)]
        return [
            start(src, kv_all.at[z, x, :, pl.ds(i * HD, HD)], to)
            for i, src in enumerate((k_in, v_in))
        ]

    def ring(s):
        if 0 < s < 4:
            for copy in hops["r", s]:
                copy.wait_recv()
        if s < 3:
            hops["r", s + 1] = block_to(-s, z_right)
        if s > 0:
            for copy in hops["l", s]:
                copy.wait_recv()
        if s < 4:
            hops["l", s + 1] = block_to(s, z_left)

    def spread(d):
        near[d] = (block_to(d, right), block_to(d, left))

    def pass_on(d):
        zb = (z + NZ + d) % NZ
        for copy in near[d][0]:
            copy.wait_recv()
        src = kv_all.at[zb, xm, pl.ds(0, h)]
        far[d] = [start(src, src, right)]
        for copy in near[d][1]:
            copy.wait_recv()
        src = kv_all.at[zb, xp, pl.ds(h, h)]
        far[d].append(start(src, src, left))

    def pack(_):
        load[2].wait()
        load[3].wait()
        for w in range(NZ):
            for g in range(GROUP):
                here = (slice(w * PIECE, (w + 1) * PIECE), slice(g * HD, (g + 1) * HD))
                there = slice(g * PIECE, (g + 1) * PIECE)
                qd_ref[w, 0, there] = q_ref[here]
                qd_ref[w, 1, there] = do_ref[here]
        qd_all[z, yh, c, yl] = qd_ref[z]

    def q_send(d):
        w = (z + NZ + d) % NZ
        pieces[d] = start(qd_ref.at[w], qd_all.at[z, yh, c, yl], device(w, y, x, c))

    def q_share(d):
        if d != 0:
            pieces[d].wait_recv()
        src = qd_all.at[(z + NZ - d) % NZ, yh, c, yl]
        q_near[d] = (start(src, src, up), start(src, src, down))

    def q_pass(d):
        zz = (z + NZ - d) % NZ
        q_near[d][0].wait_recv()
        q_near[d][1].wait_recv()
        if steps.index(d) % 2 == 0:
            src = qd_all.at[zz, ym // 2, c, ym % 2]
            q_far.append(start(src, src, up))
        else:
            src = qd_all.at[zz, yp // 2, c, yp % 2]
            q_far.append(start(src, src, down))

    def q_across(where):
        if where == 2:
            for copy in q_far:
                copy.wait_recv()
        for yy in ((y,), (yp, ym), (yo,))[where]:
            src = qd_all.at[:, yy // 2, c, yy % 2]
            ends.append(start(src, src, twin))

    def stats(stage):
        if stage == 0:
            for copy in load[4:]:
                copy.wait()
            sub = lax.broadcasted_iota(jnp.int32, (TOK, TOK), 0)
            lane = lax.broadcasted_iota(jnp.int32, (TOK, TOK), 1)
            dots = []
            for g in range(GROUP):
                cols = slice(g * HD, (g + 1) * HD)
                both = lax.dot_general(
                    do_ref[:, cols], o_ref[:, cols], (((1,), (1,)), ((), ())),
                    preferred_element_type=F32,
                )
                dots.append(jnp.sum(jnp.where(sub == lane, both, 0.0), axis=0, keepdims=True))
            numbers = jnp.concatenate([lse_ref[...]] + dots, axis=0)
            seg = seg_ref[...].astype(F32)
            sg_all[z, x] = seg
            segs = jnp.broadcast_to(seg, (2 * GROUP, TOK))
            sub, block = sub[0:8], lane[0:8] // PIECE
            turned = [
                [a if d == 0 else pltpu.roll(a, d * PIECE, 1) for d in range(NZ)]
                for a in (numbers, segs)
            ]
            for w in range(NZ):
                for i in range(2):
                    row = jnp.zeros((8, TOK), F32)
                    for d in range(NZ):
                        fits = (block == sub) & ((sub + NZ - w) % NZ == d)
                        row += jnp.where(fits, turned[i][d], 0.0)
                    st_ref[w, i:i + 1, :] = jnp.sum(row, axis=0, keepdims=True)
            st_all[z, yh, c, yl] = st_ref[z]
            few[0] = [
                start(st_ref.at[w], st_all.at[z, yh, c, yl], device(w, y, x, c)) for w in planes
            ]
            src = sg_all.at[z, x]
            few[0] += [start(src, src, device(w, y, x, c)) for w in planes]
        elif stage == 1:
            for copy in few[0]:
                copy.wait_recv()
            src = st_all.at[:, yh, c, yl]
            few[1] = [start(src, src, to) for to in (up, down, beyond)]
            src = sg_all.at[:, x]
            few[2] = [start(src, src, to) for to in (right, left, across)]
        else:
            for copy in few[1]:
                copy.wait_recv()
            src = st_all.at[:, :, c]
            few[2].append(start(src, src, twin))

    def turn(d):
        zb = (z + NZ + d) % NZ
        for copy in far[d]:
            copy.wait_recv()
        if d == 0:
            load[0].wait()
            load[1].wait()
        for i in range(NX):
            keys_t[zb, :, i * TOK:(i + 1) * TOK] = kv_all[zb, i, :, 0:HD].T

    def ranges(_):
        for copy in few[2]:
            copy.wait_recv()
        key_start, query_start, shift = origin(z, y, x, c)
        ids = lax.broadcasted_iota(jnp.int32, (IDS, TOK), 0).astype(F32)
        before = jnp.zeros((IDS, TOK), F32)
        for zz in range(NZ):
            for xx in range(NX):
                before += jnp.where(sg_all[zz, xx] < ids, 1.0, 0.0)
        before = jnp.sum(before, axis=1, keepdims=True)
        id_col = lax.broadcasted_iota(jnp.int32, (IDS, QT), 0).astype(F32)
        half = lax.broadcasted_iota(jnp.int32, (1, 128), 1) < ROWS
        lane = lax.broadcasted_iota(jnp.int32, (1, QT), 1)

        def one_tile(t, carry):
            first = t * TILE_G + shift
            g = tile_start(t, shift)

            def numbers(i, row):
                p = g + i
                return st_all[p // 8, p // 4 % 2, p // 2 % 2, p % 2, row:row + 1, :]

            def pair(a, b):
                return jnp.where(half, a, b)

            own = [numbers(i, 0) for i in range(TILE_G)]
            over = [pltpu.roll(a, ROWS, 1) for a in own]
            lse = jnp.concatenate([pair(own[0], over[1]), pair(own[2], over[3])], axis=1)
            dot = jnp.concatenate([pair(over[0], own[1]), pair(over[2], own[3])], axis=1)
            seg = [numbers(i, 1) for i in range(TILE_G)]
            seg = jnp.concatenate([pair(seg[0], seg[1]), pair(seg[2], seg[3])], axis=1)
            lo = jnp.sum(jnp.where(id_col == seg, before, 0.0), axis=0, keepdims=True)
            piece = g + lane // ROWS
            rem = piece % NZ * CHUNK + query_start + lane % PIECE - key_start
            hi = piece // NZ * CHUNK + jnp.clip(rem + 1, 0, CHUNK)
            fresh = piece >= first
            rows_ref[t, 0:1, :] = lse * LOG2E
            rows_ref[t, 1:2, :] = dot
            rows_ref[t, 2:3, :] = jnp.where(fresh, lo, float(NKEY))
            rows_ref[t, 3:4, :] = jnp.where(fresh, hi, 0).astype(F32)
            return carry

        lax.fori_loop(0, NQT, one_tile, 0)

    for do, which in [
        (spread, 0), (ring, 0), (pack, 0), (q_send, -1), (q_share, 0), (q_send, 3), (q_send, -2),
        (ring, 1), (q_send, -3), (q_send, 1), (spread, 1), (q_send, 4), (pass_on, 0),
        (spread, -1), (stats, 0), (q_share, 3), (q_share, -1), (ring, 2), (spread, -2),
        (q_send, 2), (spread, 2), (q_pass, 3), (pass_on, -1), (q_share, -2), (stats, 1),
        (q_pass, 0), (pass_on, -2), (q_share, 4), (pass_on, 1), (ring, 3), (q_share, 1),
        (spread, -3), (q_share, -3), (spread, 3), (q_share, 2), (q_pass, -2), (stats, 2),
        (turn, -2), (turn, -1), (q_pass, 1), (q_pass, 4), (q_across, 0), (q_pass, -1), (ring, 4),
        (spread, 4), (pass_on, 2), (pass_on, -3), (q_pass, -3), (q_pass, 2), (q_across, 1),
        (ranges, 0), (turn, 1), (pass_on, 3), (pass_on, 4), (q_across, 2), (turn, 2), (turn, 0),
        (turn, 3), (turn, -3), (turn, 4),
    ]:
        do(which)
    for copy in ends:
        copy.wait_recv()
    assert copies.count == N_GATHER, copies.count
    copies.finish()


def attend_kernel(
    kv_ref, qd_ref, keys_t, rows_ref, dq_acc, dk_acc, dv_acc, p_ref, ds_ref,
    low_ref, k_list, t_list, from_list,
):
    z, y, x, c = place()
    shift = origin(z, y, x, c)[2]

    def piece(t):
        return tile_start(t, shift)

    for t in range(NQT):
        low_ref[t] = jnp.min(rows_ref[t, 2:3, :]).astype(jnp.int32)

    def clear(k, carry):
        dq_acc[2 * k] = jnp.zeros((HD, QT), F32)
        dq_acc[2 * k + 1] = jnp.zeros((HD, QT), F32)
        dk_acc[k] = jnp.zeros((KT, HD), F32)
        dv_acc[k] = jnp.zeros((KT, HD), F32)
        return carry

    lax.fori_loop(0, NKT, clear, 0)

    def nothing(n):
        k_list[n] = 0
        t_list[n] = 0
        from_list[n] = -(1 << 20)

    lows = [low_ref[t] for t in range(NQT)]

    def listed(k, count):
        end = 0
        for low in lows:
            end += jnp.where(low < (k + 1) * KT, 1, 0)

        def note(t, count):
            k_list[count] = k
            t_list[count] = t
            from_list[count] = k * KT
            return count + 1

        return lax.fori_loop(2 * k + y // 2, end, note, count)

    count = lax.fori_loop(0, NKT, listed, 0)
    nothing(count)

    def sums(n, slot):
        k, t = k_list[n], t_list[n]
        q = qd_ref[pl.ds(piece(t), TILE_G), 0].reshape(QT, HD)
        do = qd_ref[pl.ds(piece(t), TILE_G), 1].reshape(QT, HD)
        p, ds = p_ref[slot], ds_ref[slot]
        dv_acc[k] += jnp.dot(p, do, preferred_element_type=F32)
        dk_acc[k] += jnp.dot(ds, q, preferred_element_type=F32)
        dq_acc[t] += jnp.dot(keys_t[k], ds, preferred_element_type=F32)

    def probabilities(n, slot):
        k, t = k_list[n], t_list[n]
        q = qd_ref[pl.ds(piece(t), TILE_G), 0].reshape(QT, HD)
        do = qd_ref[pl.ds(piece(t), TILE_G), 1].reshape(QT, HD)
        start = from_list[n].astype(F32)
        low = rows_ref[t, 2:3, :] - start
        high = rows_ref[t, 3:4, :] - start
        across = (((1,), (1,)), ((), ()))
        for i in range(KT // SUB):
            part = pl.ds(i * SUB, SUB)
            s = lax.dot_general(kv_ref[k, part, 0:HD], q, across, preferred_element_type=F32)
            dp = lax.dot_general(
                kv_ref[k, part, HD:2 * HD], do, across, preferred_element_type=F32
            )
            index = (lax.broadcasted_iota(jnp.int32, (SUB, QT), 0) + i * SUB).astype(F32)
            p = jnp.exp2(s * (SCALE * LOG2E) - rows_ref[t, 0:1, :])
            p = jnp.where((index >= low) & (index < high), p, 0.0)
            p_ref[slot, part, :] = p.astype(BF)
            ds_ref[slot, part, :] = (p * (dp - rows_ref[t, 1:2, :])).astype(BF)

    def step(i, carry):
        n = 2 * i
        sums(n, 0)
        sums(n + 1, 1)
        probabilities(n + 2, 0)
        probabilities(n + 3, 1)
        return carry

    steps = (count + 1) // 2
    probabilities(0, 0)
    probabilities(1, 1)
    lax.fori_loop(0, steps - 1, step, 0)
    sums(2 * steps - 2, 0)
    sums(2 * steps - 1, 1)


N_REDUCE = 16 + 16 + 7 + 7 + 4 + 1 + 2 + 2 + 7


def reduce_kernel(
    dq_acc, dk_acc, dv_acc, gq_ref, gk_ref, gv_ref, kv_ref, dq_in,
    far, near, out_x, ring_in, ring_out, both_in, both_out, both_sum, b_far, b_near, b_out,
    q_twin, q_sum, q_far, q_near, q_out, q_send, q_back, send, recv,
):
    z, y, x, c = place()
    xp, xm, xo = (x + 1) % NX, (x + 3) % NX, (x + 2) % NX
    yp, ym, yo = (y + 1) % NY, (y + 3) % NY, (y + 2) % NY
    zp, zm = (z + 1) % NZ, (z + NZ - 1) % NZ
    right, left = device(z, y, xp, c), device(z, y, xm, c)
    up, down = device(z, yp, x, c), device(z, ym, x, c)
    z_right, z_left = device(zp, y, x, c), device(zm, y, x, c)
    twin = device(z, y, x, 1 - c)
    planes = [(z + d) % NZ for d in range(1, NZ)]
    shift = origin(z, y, x, c)[2]

    def rounded():
        def keys_side(k, carry):
            for i in range(NX):
                part = pl.ds(i * TOK, TOK)
                kv_ref[k, i, :, 0:HD] = (dk_acc[k, part] * SCALE).astype(BF)
                kv_ref[k, i, :, HD:2 * HD] = dv_acc[k, part].astype(BF)
            return carry

        def queries_side(i, carry):
            for j in range(2):
                t = NQT - 1 - 2 * i - j
                dq = (dq_acc[t] * SCALE).astype(BF).T.reshape(TILE_G, ROWS, HD)
                for e in range(TILE_G):
                    g = tile_start(t, shift) + e
                    dq_in[g // 8, g // 4 % 2, g // 2 % 2, g % 2] = dq[e]
            return carry

        for g in range(TILE_G):
            dq_in[0, 0, g // 2, g % 2] = jnp.zeros((ROWS, HD), BF)
        lax.fori_loop(0, NQT // 2, queries_side, 0)
        lax.fori_loop(0, NKT, keys_side, 0)

    greet([right, left, up, down, twin] + [device(w, y, x, c) for w in planes], rounded)
    copies = Copies(send, recv)
    start = copies.start
    h = ROUND // 2
    rest = pl.ds(ROUND, BOTH)
    order = [4, 3, -3, 2, -2, 1, -1, 0]

    def first(n):
        zb = (z + NZ + order[n]) % NZ
        return (
            start(kv_ref.at[zb, xo, pl.ds(0, h)], far.at[n, 0], right),
            start(kv_ref.at[zb, xo, pl.ds(h, h)], far.at[n, 1], left),
        )

    def second(n, pair):
        zb = (z + NZ + order[n]) % NZ
        pair[0].wait_recv()
        out_x[n, 0, 0:h] = (kv_ref[zb, xp, 0:h].astype(F32) + far[n, 0].astype(F32)).astype(BF)
        out_x[n, 0, h:ROUND] = kv_ref[zb, xp, h:ROUND]
        a = start(out_x.at[n, 0], near.at[n, 0], right)
        pair[1].wait_recv()
        out_x[n, 1, 0:h] = kv_ref[zb, xm, 0:h]
        out_x[n, 1, h:ROUND] = (kv_ref[zb, xm, h:ROUND].astype(F32) + far[n, 1].astype(F32)).astype(BF)
        b = start(out_x.at[n, 1], near.at[n, 1], left)
        return a, b

    ring = {}

    def third(n, pair):
        off = order[n]
        zb = (z + NZ + off) % NZ
        pair[0].wait_recv()
        pair[1].wait_recv()
        total = kv_ref[zb, x, 0:ROUND].astype(F32) + near[n, 0].astype(F32) + near[n, 1].astype(F32)
        if off > 0:
            hop = 4 - off
            if hop > 0:
                ring[("r", hop)].wait_recv()
                total += ring_in[hop - 1].astype(F32)
            ring_out[n] = total.astype(BF)
            ring[("r", hop + 1)] = start(ring_out.at[n], ring_in.at[hop], z_right)
        elif off < 0:
            hop = 3 + off
            if hop > 0:
                ring[("l", hop)].wait_recv()
                total += ring_in[4 + hop - 1].astype(F32)
            ring_out[n] = total.astype(BF)
            ring[("l", hop + 1)] = start(ring_out.at[n], ring_in.at[4 + hop], z_left)
        else:
            ring[("r", 4)].wait_recv()
            ring[("l", 3)].wait_recv()
            total += ring_in[3].astype(F32) + ring_in[6].astype(F32)
            gk_ref[0:ROUND] = total[:, 0:HD].astype(BF)
            gv_ref[0:ROUND] = total[:, HD:2 * HD].astype(BF)

    def both(s):
        if s == 0:
            ring["R", 1] = start(kv_ref.at[(z + 3) % NZ, :, rest], both_in.at[0], z_right)
            ring["L", 1] = start(kv_ref.at[(z + 4) % NZ, :, rest], both_in.at[3], z_left)
            return
        if s < 4:
            ring["R", s].wait_recv()
        if s < 3:
            mine = kv_ref[(z + 3 - s) % NZ, :, ROUND:TOK].astype(F32)
            both_out[s - 1] = (mine + both_in[s - 1].astype(F32)).astype(BF)
            ring["R", s + 1] = start(both_out.at[s - 1], both_in.at[s], z_right)
        if s < 5:
            ring["L", s].wait_recv()
        if s < 4:
            mine = kv_ref[(z + 4 + s) % NZ, :, ROUND:TOK].astype(F32)
            both_out[1 + s] = (mine + both_in[2 + s].astype(F32)).astype(BF)
            ring["L", s + 1] = start(both_out.at[1 + s], both_in.at[3 + s], z_left)
        if s == 4:
            both_sum[...] = (
                kv_ref[z, :, ROUND:TOK].astype(F32)
                + both_in[2].astype(F32)
                + both_in[6].astype(F32)
            ).astype(BF)
            b = BOTH // 2
            ring["f", 0] = start(both_sum.at[xo, pl.ds(0, b)], b_far.at[0], right)
            ring["f", 1] = start(both_sum.at[xo, pl.ds(b, b)], b_far.at[1], left)
        if s == 5:
            b = BOTH // 2
            ring["f", 0].wait_recv()
            b_out[0, 0:b] = (both_sum[xp, 0:b].astype(F32) + b_far[0].astype(F32)).astype(BF)
            b_out[0, b:BOTH] = both_sum[xp, b:BOTH]
            ring["n", 0] = start(b_out.at[0], b_near.at[0], right)
            ring["f", 1].wait_recv()
            b_out[1, 0:b] = both_sum[xm, 0:b]
            b_out[1, b:BOTH] = (both_sum[xm, b:BOTH].astype(F32) + b_far[1].astype(F32)).astype(BF)
            ring["n", 1] = start(b_out.at[1], b_near.at[1], left)

    def both_end():
        ring["n", 0].wait_recv()
        ring["n", 1].wait_recv()
        total = both_sum[x].astype(F32) + b_near[0].astype(F32) + b_near[1].astype(F32)
        gk_ref[ROUND:TOK] = total[:, 0:HD].astype(BF)
        gv_ref[ROUND:TOK] = total[:, HD:2 * HD].astype(BF)

    queue = {}

    def q_step(s):
        if s == 0:
            queue["twin"] = start(dq_in.at[:, :, 1 - c], q_twin, twin)
        elif s == 1:
            queue["twin"].wait_recv()
            for zz in range(NZ):
                q_sum[zz] = (dq_in[zz, :, c].astype(F32) + q_twin[zz].astype(F32)).astype(BF)
            queue["a"] = start(q_sum.at[pl.ds(0, 4), yo // 2, yo % 2], q_far.at[0], up)
            queue["b"] = start(q_sum.at[pl.ds(4, 4), yo // 2, yo % 2], q_far.at[1], down)
        elif s == 2:
            queue["a"].wait_recv()
            q_out[0, 0:4] = (
                q_sum[0:4, yp // 2, yp % 2].astype(F32) + q_far[0].astype(F32)
            ).astype(BF)
            q_out[0, 4:8] = q_sum[4:8, yp // 2, yp % 2]
            queue["c"] = start(q_out.at[0], q_near.at[0], up)
            queue["b"].wait_recv()
            q_out[1, 0:4] = q_sum[0:4, ym // 2, ym % 2]
            q_out[1, 4:8] = (
                q_sum[4:8, ym // 2, ym % 2].astype(F32) + q_far[1].astype(F32)
            ).astype(BF)
            queue["d"] = start(q_out.at[1], q_near.at[1], down)
        else:
            queue["c"].wait_recv()
            queue["d"].wait_recv()
            q_send[...] = (
                q_sum[:, y // 2, y % 2].astype(F32)
                + q_near[0].astype(F32)
                + q_near[1].astype(F32)
            ).astype(BF)
            queue["back"] = [
                start(q_send.at[w], q_back.at[z], device(w, y, x, c)) for w in planes
            ]
            q_back[z] = q_send[z]

    one, two = {}, {}

    def x_far(n):
        one[n] = first(n)

    def x_near(n):
        two[n] = second(n, one[n])

    def x_sum(n):
        third(n, two[n])

    for do, which in [
        (q_step, 0), (x_far, 0), (both, 0), (x_far, 1), (x_far, 2), (x_far, 3), (x_near, 0),
        (x_far, 4), (x_far, 5), (both, 1), (q_step, 1), (x_near, 1), (x_near, 2), (x_sum, 0),
        (x_far, 6), (x_near, 3), (x_near, 4), (x_far, 7), (both, 2), (q_step, 2), (x_near, 5),
        (x_sum, 1), (x_sum, 2), (x_near, 6), (both, 3), (x_sum, 3), (x_sum, 4), (q_step, 3),
        (both, 4), (x_sum, 5), (x_near, 7), (x_sum, 6), (both, 5), (x_sum, 7),
    ]:
        do(which)
    both_end()
    for copy in queue["back"]:
        copy.wait_recv()
    for w in range(NZ):
        for g in range(GROUP):
            rows = slice(w * PIECE, (w + 1) * PIECE)
            gq_ref[rows, g * HD:(g + 1) * HD] = q_back[w, g * PIECE:(g + 1) * PIECE]
    assert copies.count == N_REDUCE, copies.count
    copies.finish()


def body(queries, keys, values, outputs, out_grad, log_sum_exp, segment_ids):
    hbm = pl.BlockSpec(memory_space=pltpu.HBM)
    vmem = pl.BlockSpec(memory_space=pltpu.VMEM)

    kv_all, qd_all, keys_t, row_data = pl.pallas_call(
        gather_kernel,
        out_shape=[
            jax.ShapeDtypeStruct((NZ, NX, TOK, 2 * HD), BF),
            jax.ShapeDtypeStruct((NZ, 2, NC, 2, 2, ROWS, HD), BF),
            jax.ShapeDtypeStruct((NKT, HD, KT), BF),
            jax.ShapeDtypeStruct((NQT, 8, QT), F32),
        ],
        in_specs=[hbm] * 7,
        out_specs=[vmem] * 4,
        scratch_shapes=[
            pltpu.VMEM((NZ, 2, NC, 2, 2, 128), F32),
            pltpu.VMEM((NZ, NX, 1, TOK), F32),
            pltpu.VMEM((TOK, GROUP * HD), BF),
            pltpu.VMEM((TOK, GROUP * HD), BF),
            pltpu.VMEM((TOK, GROUP * HD), BF),
            pltpu.VMEM((GROUP, TOK), F32),
            pltpu.VMEM((1, TOK), jnp.int32),
            pltpu.VMEM((NZ, 2, ROWS, HD), BF),
            pltpu.VMEM((NZ, 2, 2 * ROWS), F32),
            pltpu.SemaphoreType.DMA((N_GATHER,)),
            pltpu.SemaphoreType.DMA((N_GATHER,)),
            pltpu.SemaphoreType.DMA((7,)),
        ],
        compiler_params=pltpu.CompilerParams(
            collective_id=0, has_side_effects=True, vmem_limit_bytes=40 * 2**20
        ),
        name="gather",
    )(
        *[
            pltpu.with_memory_space_constraint(a, pltpu.HBM)
            for a in (
                queries, keys, values, outputs, out_grad,
                log_sum_exp.T, segment_ids.reshape(1, TOK),
            )
        ]
    )

    sums = pl.pallas_call(
        attend_kernel,
        out_shape=[
            jax.ShapeDtypeStruct((NQT, HD, QT), F32),
            jax.ShapeDtypeStruct((NKT, KT, HD), F32),
            jax.ShapeDtypeStruct((NKT, KT, HD), F32),
        ],
        in_specs=[vmem] * 4,
        out_specs=[vmem] * 3,
        scratch_shapes=[
            pltpu.VMEM((2, KT, QT), BF),
            pltpu.VMEM((2, KT, QT), BF),
            pltpu.SMEM((NQT,), jnp.int32),
            pltpu.SMEM((STEPS,), jnp.int32),
            pltpu.SMEM((STEPS,), jnp.int32),
            pltpu.SMEM((STEPS,), jnp.int32),
        ],
        compiler_params=pltpu.CompilerParams(vmem_limit_bytes=40 * 2**20),
        name="attend",
    )(
        kv_all.reshape(NKT, KT, 2 * HD),
        qd_all.reshape(NG, 2, ROWS, HD),
        keys_t,
        row_data,
    )

    return pl.pallas_call(
        reduce_kernel,
        out_shape=[
            jax.ShapeDtypeStruct((TOK, GROUP * HD), BF),
            jax.ShapeDtypeStruct((TOK, HD), BF),
            jax.ShapeDtypeStruct((TOK, HD), BF),
        ],
        in_specs=[vmem] * 3,
        out_specs=[vmem] * 3,
        scratch_shapes=[
            pltpu.VMEM((NZ, NX, TOK, 2 * HD), BF),
            pltpu.VMEM((NZ, 2, NC, 2, ROWS, HD), BF),
            pltpu.VMEM((NZ, 2, ROUND // 2, 2 * HD), BF),
            pltpu.VMEM((NZ, 2, ROUND, 2 * HD), BF),
            pltpu.VMEM((NZ, 2, ROUND, 2 * HD), BF),
            pltpu.VMEM((7, ROUND, 2 * HD), BF),
            pltpu.VMEM((7, ROUND, 2 * HD), BF),
            pltpu.VMEM((7, NX, BOTH, 2 * HD), BF),
            pltpu.VMEM((5, NX, BOTH, 2 * HD), BF),
            pltpu.VMEM((NX, BOTH, 2 * HD), BF),
            pltpu.VMEM((2, BOTH // 2, 2 * HD), BF),
            pltpu.VMEM((2, BOTH, 2 * HD), BF),
            pltpu.VMEM((2, BOTH, 2 * HD), BF),
            pltpu.VMEM((NZ, 2, 2, ROWS, HD), BF),
            pltpu.VMEM((NZ, 2, 2, ROWS, HD), BF),
            pltpu.VMEM((2, 4, ROWS, HD), BF),
            pltpu.VMEM((2, NZ, ROWS, HD), BF),
            pltpu.VMEM((2, NZ, ROWS, HD), BF),
            pltpu.VMEM((NZ, ROWS, HD), BF),
            pltpu.VMEM((NZ, ROWS, HD), BF),
            pltpu.SemaphoreType.DMA((N_REDUCE,)),
            pltpu.SemaphoreType.DMA((N_REDUCE,)),
        ],
        compiler_params=pltpu.CompilerParams(
            collective_id=1, has_side_effects=True, vmem_limit_bytes=40 * 2**20
        ),
        name="reduce",
    )(*sums)


def solution(mesh):
    rows = P(("row", "col"), None)
    return jax.shard_map(
        body,
        mesh=mesh,
        in_specs=(rows, rows, rows, rows, rows, rows, P(("row", "col"))),
        out_specs=(rows, rows, rows),
        check_vma=False,
    )
```

```python
import functools
import math

import jax
import jax.numpy as jnp
from jax import lax
from jax.experimental import pallas as pl
from jax.experimental.pallas import tpu as pltpu
from jax.sharding import PartitionSpec as P

MESH = pl.DeviceIdType.MESH
HD = 128
GROUP = 4
NZ, NY, NX, NC = 8, 4, 4, 2
TOK = 128
PIECE = TOK // NZ
ROWS = PIECE * GROUP
NG = NZ * NY * NC
TILE_G = 4
NQT = NG // TILE_G
QT = TILE_G * ROWS
KT = 512
SUB = 256
ROUND = 96
BOTH = TOK - ROUND
NKEY = NZ * NX * TOK
NKT = NKEY // KT
CHUNK = NX * TOK
IDS = 72
STEPS = NQT * NKT + 8
SCALE = HD ** -0.5
LOG2E = math.log2(math.e)
BF = jnp.bfloat16
F32 = jnp.float32


def place():
    row = lax.axis_index("row")
    col = lax.axis_index("col")
    z = row // 4
    y = (row // 2) % 2 * 2 + col // 4
    return z, y, col % 4, row % 2


def device(z, y, x, c):
    return (z * 4 + y // 2 * 2 + c, y % 2 * 4 + x)


def origin(z, y, x, c):
    return y // 2 * 2048 + c * 1024 + y % 2 * 512, x * TOK + z * PIECE, c * 2 + y % 2


def tile_start(t, shift):
    return jnp.minimum(t * TILE_G + shift, NG - TILE_G)


class Copies:
    def __init__(self, send, recv):
        self.send, self.recv, self.count, self.all = send, recv, 0, []

    def start(self, src, dst, to):
        i = self.count
        self.count += 1
        copy = pltpu.make_async_remote_copy(
            src_ref=src,
            dst_ref=dst,
            send_sem=self.send.at[i],
            recv_sem=self.recv.at[i],
            device_id=to,
            device_id_type=MESH,
        )
        copy.start()
        self.all.append(copy)
        return copy

    def finish(self):
        for copy in self.all:
            copy.wait_send()


def greet(peers, meanwhile=None):
    barrier = pltpu.get_barrier_semaphore()
    for peer in peers:
        pl.semaphore_signal(barrier, inc=1, device_id=peer, device_id_type=MESH)
    if meanwhile is not None:
        meanwhile()
    pl.semaphore_wait(barrier, len(peers))


N_GATHER = 34 + 9 + 7 + 24 + 4 + 11 + 10


def gather_kernel(
    q_in, k_in, v_in, o_in, do_in, lse_in, seg_in, kv_all, qd_all, keys_t, rows_ref,
    st_all, sg_all, q_ref, o_ref, do_ref, lse_ref, seg_ref, qd_ref, st_ref, send, recv, local,
):
    z, y, x, c = place()
    xp, xm, xo = (x + 1) % NX, (x + 3) % NX, (x + 2) % NX
    yp, ym, yo = (y + 1) % NY, (y + 3) % NY, (y + 2) % NY
    zp, zm = (z + 1) % NZ, (z + NZ - 1) % NZ
    right, left, across = device(z, y, xp, c), device(z, y, xm, c), device(z, y, xo, c)
    up, down, beyond = device(z, yp, x, c), device(z, ym, x, c), device(z, yo, x, c)
    z_right, z_left = device(zp, y, x, c), device(zm, y, x, c)
    twin = device(z, y, x, 1 - c)
    planes = [(z + d) % NZ for d in range(1, NZ)]
    load = [
        pltpu.make_async_copy(src, dst, local.at[i])
        for i, (src, dst) in enumerate([
            (k_in, kv_all.at[z, x, :, pl.ds(0, HD)]),
            (v_in, kv_all.at[z, x, :, pl.ds(HD, HD)]),
            (q_in, q_ref),
            (do_in, do_ref),
            (o_in, o_ref),
            (lse_in, lse_ref),
            (seg_in, seg_ref),
        ])
    ]
    for copy in load:
        copy.start()
    greet(
        [right, left, across, up, down, beyond, twin] + [device(w, y, x, c) for w in planes]
    )
    copies = Copies(send, recv)
    start = copies.start
    yh, yl = y // 2, y % 2

    near, far, hops, pieces, q_near, q_far = {}, {}, {}, {}, {}, []
    few, ends = {}, []
    steps = [0, 1, -1, 2, -2, 3, -3, 4]
    h = TOK // 2

    def block_to(d, to):
        if d != 0:
            src = kv_all.at[(z + NZ + d) % NZ, x]
            return [start(src, src, to)]
        return [
            start(src, kv_all.at[z, x, :, pl.ds(i * HD, HD)], to)
            for i, src in enumerate((k_in, v_in))
        ]

    def ring(s):
        if 0 < s < 4:
            for copy in hops["r", s]:
                copy.wait_recv()
        if s < 3:
            hops["r", s + 1] = block_to(-s, z_right)
        if s > 0:
            for copy in hops["l", s]:
                copy.wait_recv()
        if s < 4:
            hops["l", s + 1] = block_to(s, z_left)

    def spread(d):
        near[d] = (block_to(d, right), block_to(d, left))

    def pass_on(d):
        zb = (z + NZ + d) % NZ
        for copy in near[d][0]:
            copy.wait_recv()
        src = kv_all.at[zb, xm, pl.ds(0, h)]
        far[d] = [start(src, src, right)]
        for copy in near[d][1]:
            copy.wait_recv()
        src = kv_all.at[zb, xp, pl.ds(h, h)]
        far[d].append(start(src, src, left))

    def pack(_):
        load[2].wait()
        load[3].wait()
        for w in range(NZ):
            for g in range(GROUP):
                here = (slice(w * PIECE, (w + 1) * PIECE), slice(g * HD, (g + 1) * HD))
                there = slice(g * PIECE, (g + 1) * PIECE)
                qd_ref[w, 0, there] = q_ref[here]
                qd_ref[w, 1, there] = do_ref[here]
        qd_all[z, yh, c, yl] = qd_ref[z]

    def q_send(d):
        w = (z + NZ + d) % NZ
        pieces[d] = start(qd_ref.at[w], qd_all.at[z, yh, c, yl], device(w, y, x, c))

    def q_share(d):
        if d != 0:
            pieces[d].wait_recv()
        src = qd_all.at[(z + NZ - d) % NZ, yh, c, yl]
        q_near[d] = (start(src, src, up), start(src, src, down))

    def q_pass(d):
        zz = (z + NZ - d) % NZ
        q_near[d][0].wait_recv()
        q_near[d][1].wait_recv()
        if steps.index(d) % 2 == 0:
            src = qd_all.at[zz, ym // 2, c, ym % 2]
            q_far.append(start(src, src, up))
        else:
            src = qd_all.at[zz, yp // 2, c, yp % 2]
            q_far.append(start(src, src, down))

    def q_across(where):
        if where == 2:
            for copy in q_far:
                copy.wait_recv()
        for yy in ((y,), (yp, ym), (yo,))[where]:
            src = qd_all.at[:, yy // 2, c, yy % 2]
            ends.append(start(src, src, twin))

    def stats(stage):
        if stage == 0:
            for copy in load[4:]:
                copy.wait()
            sub = lax.broadcasted_iota(jnp.int32, (TOK, TOK), 0)
            lane = lax.broadcasted_iota(jnp.int32, (TOK, TOK), 1)
            dots = []
            for g in range(GROUP):
                cols = slice(g * HD, (g + 1) * HD)
                both = lax.dot_general(
                    do_ref[:, cols], o_ref[:, cols], (((1,), (1,)), ((), ())),
                    preferred_element_type=F32,
                )
                dots.append(jnp.sum(jnp.where(sub == lane, both, 0.0), axis=0, keepdims=True))
            numbers = jnp.concatenate([lse_ref[...]] + dots, axis=0)
            seg = seg_ref[...].astype(F32)
            sg_all[z, x] = seg
            segs = jnp.broadcast_to(seg, (2 * GROUP, TOK))
            sub, block = sub[0:8], lane[0:8] // PIECE
            turned = [
                [a if d == 0 else pltpu.roll(a, d * PIECE, 1) for d in range(NZ)]
                for a in (numbers, segs)
            ]
            for w in range(NZ):
                for i in range(2):
                    row = jnp.zeros((8, TOK), F32)
                    for d in range(NZ):
                        fits = (block == sub) & ((sub + NZ - w) % NZ == d)
                        row += jnp.where(fits, turned[i][d], 0.0)
                    st_ref[w, i:i + 1, :] = jnp.sum(row, axis=0, keepdims=True)
            st_all[z, yh, c, yl] = st_ref[z]
            few[0] = [
                start(st_ref.at[w], st_all.at[z, yh, c, yl], device(w, y, x, c)) for w in planes
            ]
            src = sg_all.at[z, x]
            few[0] += [start(src, src, device(w, y, x, c)) for w in planes]
        elif stage == 1:
            for copy in few[0]:
                copy.wait_recv()
            src = st_all.at[:, yh, c, yl]
            few[1] = [start(src, src, to) for to in (up, down, beyond)]
            src = sg_all.at[:, x]
            few[2] = [start(src, src, to) for to in (right, left, across)]
        else:
            for copy in few[1]:
                copy.wait_recv()
            src = st_all.at[:, :, c]
            few[2].append(start(src, src, twin))

    def turn(d):
        zb = (z + NZ + d) % NZ
        for copy in far[d]:
            copy.wait_recv()
        if d == 0:
            load[0].wait()
            load[1].wait()
        for i in range(NX):
            keys_t[zb, :, i * TOK:(i + 1) * TOK] = kv_all[zb, i, :, 0:HD].T

    def ranges(_):
        for copy in few[2]:
            copy.wait_recv()
        key_start, query_start, shift = origin(z, y, x, c)
        ids = lax.broadcasted_iota(jnp.int32, (IDS, TOK), 0).astype(F32)
        before = jnp.zeros((IDS, TOK), F32)
        for zz in range(NZ):
            for xx in range(NX):
                before += jnp.where(sg_all[zz, xx] < ids, 1.0, 0.0)
        before = jnp.sum(before, axis=1, keepdims=True)
        id_col = lax.broadcasted_iota(jnp.int32, (IDS, QT), 0).astype(F32)
        half = lax.broadcasted_iota(jnp.int32, (1, 128), 1) < ROWS
        lane = lax.broadcasted_iota(jnp.int32, (1, QT), 1)

        def one_tile(t, carry):
            first = t * TILE_G + shift
            g = tile_start(t, shift)

            def numbers(i, row):
                p = g + i
                return st_all[p // 8, p // 4 % 2, p // 2 % 2, p % 2, row:row + 1, :]

            def pair(a, b):
                return jnp.where(half, a, b)

            own = [numbers(i, 0) for i in range(TILE_G)]
            over = [pltpu.roll(a, ROWS, 1) for a in own]
            lse = jnp.concatenate([pair(own[0], over[1]), pair(own[2], over[3])], axis=1)
            dot = jnp.concatenate([pair(over[0], own[1]), pair(over[2], own[3])], axis=1)
            seg = [numbers(i, 1) for i in range(TILE_G)]
            seg = jnp.concatenate([pair(seg[0], seg[1]), pair(seg[2], seg[3])], axis=1)
            lo = jnp.sum(jnp.where(id_col == seg, before, 0.0), axis=0, keepdims=True)
            piece = g + lane // ROWS
            rem = piece % NZ * CHUNK + query_start + lane % PIECE - key_start
            hi = piece // NZ * CHUNK + jnp.clip(rem + 1, 0, CHUNK)
            fresh = piece >= first
            rows_ref[t, 0:1, :] = lse * LOG2E
            rows_ref[t, 1:2, :] = dot
            rows_ref[t, 2:3, :] = jnp.where(fresh, lo, float(NKEY))
            rows_ref[t, 3:4, :] = jnp.where(fresh, hi, 0).astype(F32)
            return carry

        lax.fori_loop(0, NQT, one_tile, 0)

    for do, which in [
        (spread, 0), (ring, 0), (pack, 0), (q_send, -1), (q_share, 0), (q_send, 3), (q_send, -2),
        (ring, 1), (q_send, -3), (q_send, 1), (spread, 1), (q_send, 4), (pass_on, 0),
        (spread, -1), (stats, 0), (q_share, 3), (q_share, -1), (ring, 2), (spread, -2),
        (q_send, 2), (spread, 2), (q_pass, 3), (pass_on, -1), (q_share, -2), (stats, 1),
        (q_pass, 0), (pass_on, -2), (q_share, 4), (pass_on, 1), (ring, 3), (q_share, 1),
        (spread, -3), (q_share, -3), (spread, 3), (q_share, 2), (q_pass, -2), (stats, 2),
        (turn, -2), (turn, -1), (q_pass, 1), (q_pass, 4), (q_across, 0), (q_pass, -1), (ring, 4),
        (spread, 4), (pass_on, 2), (pass_on, -3), (q_pass, -3), (q_pass, 2), (q_across, 1),
        (ranges, 0), (turn, 1), (pass_on, 3), (pass_on, 4), (q_across, 2), (turn, 2), (turn, 0),
        (turn, 3), (turn, -3), (turn, 4),
    ]:
        do(which)
    for copy in ends:
        copy.wait_recv()
    assert copies.count == N_GATHER, copies.count
    copies.finish()


def attend_kernel(
    kv_ref, qd_ref, keys_t, rows_ref, dq_acc, dk_acc, dv_acc, p_ref, ds_ref,
    low_ref, k_list, t_list, from_list,
):
    z, y, x, c = place()
    shift = origin(z, y, x, c)[2]

    def piece(t):
        return tile_start(t, shift)

    for t in range(NQT):
        low_ref[t] = jnp.min(rows_ref[t, 2:3, :]).astype(jnp.int32)

    def clear(k, carry):
        dq_acc[2 * k] = jnp.zeros((HD, QT), F32)
        dq_acc[2 * k + 1] = jnp.zeros((HD, QT), F32)
        dk_acc[k] = jnp.zeros((KT, HD), F32)
        dv_acc[k] = jnp.zeros((KT, HD), F32)
        return carry

    lax.fori_loop(0, NKT, clear, 0)

    def nothing(n):
        k_list[n] = 0
        t_list[n] = 0
        from_list[n] = -(1 << 20)

    lows = [low_ref[t] for t in range(NQT)]

    def listed(k, count):
        end = 0
        for low in lows:
            end += jnp.where(low < (k + 1) * KT, 1, 0)

        def note(t, count):
            k_list[count] = k
            t_list[count] = t
            from_list[count] = k * KT
            return count + 1

        return lax.fori_loop(2 * k + y // 2, end, note, count)

    count = lax.fori_loop(0, NKT, listed, 0)
    nothing(count)

    def sums(n, slot):
        k, t = k_list[n], t_list[n]
        q = qd_ref[pl.ds(piece(t), TILE_G), 0].reshape(QT, HD)
        do = qd_ref[pl.ds(piece(t), TILE_G), 1].reshape(QT, HD)
        p, ds = p_ref[slot], ds_ref[slot]
        dv_acc[k] += jnp.dot(p, do, preferred_element_type=F32)
        dk_acc[k] += jnp.dot(ds, q, preferred_element_type=F32)
        dq_acc[t] += jnp.dot(keys_t[k], ds, preferred_element_type=F32)

    def probabilities(n, slot):
        k, t = k_list[n], t_list[n]
        q = qd_ref[pl.ds(piece(t), TILE_G), 0].reshape(QT, HD)
        do = qd_ref[pl.ds(piece(t), TILE_G), 1].reshape(QT, HD)
        start = from_list[n].astype(F32)
        low = rows_ref[t, 2:3, :] - start
        high = rows_ref[t, 3:4, :] - start
        across = (((1,), (1,)), ((), ()))
        for i in range(KT // SUB):
            part = pl.ds(i * SUB, SUB)
            s = lax.dot_general(kv_ref[k, part, 0:HD], q, across, preferred_element_type=F32)
            dp = lax.dot_general(
                kv_ref[k, part, HD:2 * HD], do, across, preferred_element_type=F32
            )
            index = (lax.broadcasted_iota(jnp.int32, (SUB, QT), 0) + i * SUB).astype(F32)
            p = jnp.exp2(s * (SCALE * LOG2E) - rows_ref[t, 0:1, :])
            p = jnp.where((index >= low) & (index < high), p, 0.0)
            p_ref[slot, part, :] = p.astype(BF)
            ds_ref[slot, part, :] = (p * (dp - rows_ref[t, 1:2, :])).astype(BF)

    def step(i, carry):
        n = 2 * i
        sums(n, 0)
        sums(n + 1, 1)
        probabilities(n + 2, 0)
        probabilities(n + 3, 1)
        return carry

    steps = (count + 1) // 2
    probabilities(0, 0)
    probabilities(1, 1)
    lax.fori_loop(0, steps - 1, step, 0)
    sums(2 * steps - 2, 0)
    sums(2 * steps - 1, 1)


N_REDUCE = 16 + 16 + 7 + 7 + 4 + 1 + 2 + 2 + 7


def reduce_kernel(
    dq_acc, dk_acc, dv_acc, gq_ref, gk_ref, gv_ref, kv_ref, dq_in,
    far, near, out_x, ring_in, ring_out, both_in, both_out, both_sum, b_far, b_near, b_out,
    q_twin, q_sum, q_far, q_near, q_out, q_send, q_back, send, recv,
):
    z, y, x, c = place()
    xp, xm, xo = (x + 1) % NX, (x + 3) % NX, (x + 2) % NX
    yp, ym, yo = (y + 1) % NY, (y + 3) % NY, (y + 2) % NY
    zp, zm = (z + 1) % NZ, (z + NZ - 1) % NZ
    right, left = device(z, y, xp, c), device(z, y, xm, c)
    up, down = device(z, yp, x, c), device(z, ym, x, c)
    z_right, z_left = device(zp, y, x, c), device(zm, y, x, c)
    twin = device(z, y, x, 1 - c)
    planes = [(z + d) % NZ for d in range(1, NZ)]
    shift = origin(z, y, x, c)[2]

    def rounded():
        def keys_side(k, carry):
            for i in range(NX):
                part = pl.ds(i * TOK, TOK)
                kv_ref[k, i, :, 0:HD] = (dk_acc[k, part] * SCALE).astype(BF)
                kv_ref[k, i, :, HD:2 * HD] = dv_acc[k, part].astype(BF)
            return carry

        def queries_side(i, carry):
            for j in range(2):
                t = NQT - 1 - 2 * i - j
                dq = (dq_acc[t] * SCALE).astype(BF).T.reshape(TILE_G, ROWS, HD)
                for e in range(TILE_G):
                    g = tile_start(t, shift) + e
                    dq_in[g // 8, g // 4 % 2, g // 2 % 2, g % 2] = dq[e]
            return carry

        for g in range(TILE_G):
            dq_in[0, 0, g // 2, g % 2] = jnp.zeros((ROWS, HD), BF)
        lax.fori_loop(0, NQT // 2, queries_side, 0)
        lax.fori_loop(0, NKT, keys_side, 0)

    greet([right, left, up, down, twin] + [device(w, y, x, c) for w in planes], rounded)
    copies = Copies(send, recv)
    start = copies.start
    h = ROUND // 2
    rest = pl.ds(ROUND, BOTH)
    order = [4, 3, -3, 2, -2, 1, -1, 0]

    def first(n):
        zb = (z + NZ + order[n]) % NZ
        return (
            start(kv_ref.at[zb, xo, pl.ds(0, h)], far.at[n, 0], right),
            start(kv_ref.at[zb, xo, pl.ds(h, h)], far.at[n, 1], left),
        )

    def second(n, pair):
        zb = (z + NZ + order[n]) % NZ
        pair[0].wait_recv()
        out_x[n, 0, 0:h] = (kv_ref[zb, xp, 0:h].astype(F32) + far[n, 0].astype(F32)).astype(BF)
        out_x[n, 0, h:ROUND] = kv_ref[zb, xp, h:ROUND]
        a = start(out_x.at[n, 0], near.at[n, 0], right)
        pair[1].wait_recv()
        out_x[n, 1, 0:h] = kv_ref[zb, xm, 0:h]
        out_x[n, 1, h:ROUND] = (kv_ref[zb, xm, h:ROUND].astype(F32) + far[n, 1].astype(F32)).astype(BF)
        b = start(out_x.at[n, 1], near.at[n, 1], left)
        return a, b

    ring = {}

    def third(n, pair):
        off = order[n]
        zb = (z + NZ + off) % NZ
        pair[0].wait_recv()
        pair[1].wait_recv()
        total = kv_ref[zb, x, 0:ROUND].astype(F32) + near[n, 0].astype(F32) + near[n, 1].astype(F32)
        if off > 0:
            hop = 4 - off
            if hop > 0:
                ring[("r", hop)].wait_recv()
                total += ring_in[hop - 1].astype(F32)
            ring_out[n] = total.astype(BF)
            ring[("r", hop + 1)] = start(ring_out.at[n], ring_in.at[hop], z_right)
        elif off < 0:
            hop = 3 + off
            if hop > 0:
                ring[("l", hop)].wait_recv()
                total += ring_in[4 + hop - 1].astype(F32)
            ring_out[n] = total.astype(BF)
            ring[("l", hop + 1)] = start(ring_out.at[n], ring_in.at[4 + hop], z_left)
        else:
            ring[("r", 4)].wait_recv()
            ring[("l", 3)].wait_recv()
            total += ring_in[3].astype(F32) + ring_in[6].astype(F32)
            gk_ref[0:ROUND] = total[:, 0:HD].astype(BF)
            gv_ref[0:ROUND] = total[:, HD:2 * HD].astype(BF)

    def both(s):
        if s == 0:
            ring["R", 1] = start(kv_ref.at[(z + 3) % NZ, :, rest], both_in.at[0], z_right)
            ring["L", 1] = start(kv_ref.at[(z + 4) % NZ, :, rest], both_in.at[3], z_left)
            return
        if s < 4:
            ring["R", s].wait_recv()
        if s < 3:
            mine = kv_ref[(z + 3 - s) % NZ, :, ROUND:TOK].astype(F32)
            both_out[s - 1] = (mine + both_in[s - 1].astype(F32)).astype(BF)
            ring["R", s + 1] = start(both_out.at[s - 1], both_in.at[s], z_right)
        if s < 5:
            ring["L", s].wait_recv()
        if s < 4:
            mine = kv_ref[(z + 4 + s) % NZ, :, ROUND:TOK].astype(F32)
            both_out[1 + s] = (mine + both_in[2 + s].astype(F32)).astype(BF)
            ring["L", s + 1] = start(both_out.at[1 + s], both_in.at[3 + s], z_left)
        if s == 4:
            both_sum[...] = (
                kv_ref[z, :, ROUND:TOK].astype(F32)
                + both_in[2].astype(F32)
                + both_in[6].astype(F32)
            ).astype(BF)
            b = BOTH // 2
            ring["f", 0] = start(both_sum.at[xo, pl.ds(0, b)], b_far.at[0], right)
            ring["f", 1] = start(both_sum.at[xo, pl.ds(b, b)], b_far.at[1], left)
        if s == 5:
            b = BOTH // 2
            ring["f", 0].wait_recv()
            b_out[0, 0:b] = (both_sum[xp, 0:b].astype(F32) + b_far[0].astype(F32)).astype(BF)
            b_out[0, b:BOTH] = both_sum[xp, b:BOTH]
            ring["n", 0] = start(b_out.at[0], b_near.at[0], right)
            ring["f", 1].wait_recv()
            b_out[1, 0:b] = both_sum[xm, 0:b]
            b_out[1, b:BOTH] = (both_sum[xm, b:BOTH].astype(F32) + b_far[1].astype(F32)).astype(BF)
            ring["n", 1] = start(b_out.at[1], b_near.at[1], left)

    def both_end():
        ring["n", 0].wait_recv()
        ring["n", 1].wait_recv()
        total = both_sum[x].astype(F32) + b_near[0].astype(F32) + b_near[1].astype(F32)
        gk_ref[ROUND:TOK] = total[:, 0:HD].astype(BF)
        gv_ref[ROUND:TOK] = total[:, HD:2 * HD].astype(BF)

    queue = {}

    def q_step(s):
        if s == 0:
            queue["twin"] = start(dq_in.at[:, :, 1 - c], q_twin, twin)
        elif s == 1:
            queue["twin"].wait_recv()
            for zz in range(NZ):
                q_sum[zz] = (dq_in[zz, :, c].astype(F32) + q_twin[zz].astype(F32)).astype(BF)
            queue["a"] = start(q_sum.at[pl.ds(0, 4), yo // 2, yo % 2], q_far.at[0], up)
            queue["b"] = start(q_sum.at[pl.ds(4, 4), yo // 2, yo % 2], q_far.at[1], down)
        elif s == 2:
            queue["a"].wait_recv()
            q_out[0, 0:4] = (
                q_sum[0:4, yp // 2, yp % 2].astype(F32) + q_far[0].astype(F32)
            ).astype(BF)
            q_out[0, 4:8] = q_sum[4:8, yp // 2, yp % 2]
            queue["c"] = start(q_out.at[0], q_near.at[0], up)
            queue["b"].wait_recv()
            q_out[1, 0:4] = q_sum[0:4, ym // 2, ym % 2]
            q_out[1, 4:8] = (
                q_sum[4:8, ym // 2, ym % 2].astype(F32) + q_far[1].astype(F32)
            ).astype(BF)
            queue["d"] = start(q_out.at[1], q_near.at[1], down)
        else:
            queue["c"].wait_recv()
            queue["d"].wait_recv()
            q_send[...] = (
                q_sum[:, y // 2, y % 2].astype(F32)
                + q_near[0].astype(F32)
                + q_near[1].astype(F32)
            ).astype(BF)
            queue["back"] = [
                start(q_send.at[w], q_back.at[z], device(w, y, x, c)) for w in planes
            ]
            q_back[z] = q_send[z]

    one, two = {}, {}

    def x_far(n):
        one[n] = first(n)

    def x_near(n):
        two[n] = second(n, one[n])

    def x_sum(n):
        third(n, two[n])

    for do, which in [
        (x_far, 0), (both, 0), (x_far, 1), (x_far, 2), (x_far, 3), (q_step, 0), (x_near, 0),
        (x_far, 4), (x_far, 5), (both, 1), (x_near, 1), (q_step, 1), (x_near, 2), (x_sum, 0),
        (x_far, 6), (x_near, 3), (x_near, 4), (x_far, 7), (both, 2), (q_step, 2), (x_near, 5),
        (x_sum, 1), (x_sum, 2), (x_near, 6), (both, 3), (x_sum, 3), (x_sum, 4), (q_step, 3),
        (both, 4), (x_sum, 5), (x_near, 7), (x_sum, 6), (both, 5), (x_sum, 7),
    ]:
        do(which)
    both_end()
    for copy in queue["back"]:
        copy.wait_recv()
    for w in range(NZ):
        for g in range(GROUP):
            rows = slice(w * PIECE, (w + 1) * PIECE)
            gq_ref[rows, g * HD:(g + 1) * HD] = q_back[w, g * PIECE:(g + 1) * PIECE]
    assert copies.count == N_REDUCE, copies.count
    copies.finish()


def body(queries, keys, values, outputs, out_grad, log_sum_exp, segment_ids):
    hbm = pl.BlockSpec(memory_space=pltpu.HBM)
    vmem = pl.BlockSpec(memory_space=pltpu.VMEM)

    kv_all, qd_all, keys_t, row_data = pl.pallas_call(
        gather_kernel,
        out_shape=[
            jax.ShapeDtypeStruct((NZ, NX, TOK, 2 * HD), BF),
            jax.ShapeDtypeStruct((NZ, 2, NC, 2, 2, ROWS, HD), BF),
            jax.ShapeDtypeStruct((NKT, HD, KT), BF),
            jax.ShapeDtypeStruct((NQT, 8, QT), F32),
        ],
        in_specs=[hbm] * 7,
        out_specs=[vmem] * 4,
        scratch_shapes=[
            pltpu.VMEM((NZ, 2, NC, 2, 2, 128), F32),
            pltpu.VMEM((NZ, NX, 1, TOK), F32),
            pltpu.VMEM((TOK, GROUP * HD), BF),
            pltpu.VMEM((TOK, GROUP * HD), BF),
            pltpu.VMEM((TOK, GROUP * HD), BF),
            pltpu.VMEM((GROUP, TOK), F32),
            pltpu.VMEM((1, TOK), jnp.int32),
            pltpu.VMEM((NZ, 2, ROWS, HD), BF),
            pltpu.VMEM((NZ, 2, 2 * ROWS), F32),
            pltpu.SemaphoreType.DMA((N_GATHER,)),
            pltpu.SemaphoreType.DMA((N_GATHER,)),
            pltpu.SemaphoreType.DMA((7,)),
        ],
        compiler_params=pltpu.CompilerParams(
            collective_id=0, has_side_effects=True, vmem_limit_bytes=40 * 2**20
        ),
        name="gather",
    )(
        *[
            pltpu.with_memory_space_constraint(a, pltpu.HBM)
            for a in (
                queries, keys, values, outputs, out_grad,
                log_sum_exp.T, segment_ids.reshape(1, TOK),
            )
        ]
    )

    sums = pl.pallas_call(
        attend_kernel,
        out_shape=[
            jax.ShapeDtypeStruct((NQT, HD, QT), F32),
            jax.ShapeDtypeStruct((NKT, KT, HD), F32),
            jax.ShapeDtypeStruct((NKT, KT, HD), F32),
        ],
        in_specs=[vmem] * 4,
        out_specs=[vmem] * 3,
        scratch_shapes=[
            pltpu.VMEM((2, KT, QT), BF),
            pltpu.VMEM((2, KT, QT), BF),
            pltpu.SMEM((NQT,), jnp.int32),
            pltpu.SMEM((STEPS,), jnp.int32),
            pltpu.SMEM((STEPS,), jnp.int32),
            pltpu.SMEM((STEPS,), jnp.int32),
        ],
        compiler_params=pltpu.CompilerParams(vmem_limit_bytes=40 * 2**20),
        name="attend",
    )(
        kv_all.reshape(NKT, KT, 2 * HD),
        qd_all.reshape(NG, 2, ROWS, HD),
        keys_t,
        row_data,
    )

    return pl.pallas_call(
        reduce_kernel,
        out_shape=[
            jax.ShapeDtypeStruct((TOK, GROUP * HD), BF),
            jax.ShapeDtypeStruct((TOK, HD), BF),
            jax.ShapeDtypeStruct((TOK, HD), BF),
        ],
        in_specs=[vmem] * 3,
        out_specs=[vmem] * 3,
        scratch_shapes=[
            pltpu.VMEM((NZ, NX, TOK, 2 * HD), BF),
            pltpu.VMEM((NZ, 2, NC, 2, ROWS, HD), BF),
            pltpu.VMEM((NZ, 2, ROUND // 2, 2 * HD), BF),
            pltpu.VMEM((NZ, 2, ROUND, 2 * HD), BF),
            pltpu.VMEM((NZ, 2, ROUND, 2 * HD), BF),
            pltpu.VMEM((7, ROUND, 2 * HD), BF),
            pltpu.VMEM((7, ROUND, 2 * HD), BF),
            pltpu.VMEM((7, NX, BOTH, 2 * HD), BF),
            pltpu.VMEM((5, NX, BOTH, 2 * HD), BF),
            pltpu.VMEM((NX, BOTH, 2 * HD), BF),
            pltpu.VMEM((2, BOTH // 2, 2 * HD), BF),
            pltpu.VMEM((2, BOTH, 2 * HD), BF),
            pltpu.VMEM((2, BOTH, 2 * HD), BF),
            pltpu.VMEM((NZ, 2, 2, ROWS, HD), BF),
            pltpu.VMEM((NZ, 2, 2, ROWS, HD), BF),
            pltpu.VMEM((2, 4, ROWS, HD), BF),
            pltpu.VMEM((2, NZ, ROWS, HD), BF),
            pltpu.VMEM((2, NZ, ROWS, HD), BF),
            pltpu.VMEM((NZ, ROWS, HD), BF),
            pltpu.VMEM((NZ, ROWS, HD), BF),
            pltpu.SemaphoreType.DMA((N_REDUCE,)),
            pltpu.SemaphoreType.DMA((N_REDUCE,)),
        ],
        compiler_params=pltpu.CompilerParams(
            collective_id=1, has_side_effects=True, vmem_limit_bytes=40 * 2**20
        ),
        name="reduce",
    )(*sums)


def solution(mesh):
    rows = P(("row", "col"), None)
    return jax.shard_map(
        body,
        mesh=mesh,
        in_specs=(rows, rows, rows, rows, rows, rows, P(("row", "col"))),
        out_specs=(rows, rows, rows),
        check_vma=False,
    )
```

```python
import functools
import math

import jax
import jax.numpy as jnp
from jax import lax
from jax.experimental import pallas as pl
from jax.experimental.pallas import tpu as pltpu
from jax.sharding import PartitionSpec as P

MESH = pl.DeviceIdType.MESH
HD = 128
GROUP = 4
NZ, NY, NX, NC = 8, 4, 4, 2
TOK = 128
PIECE = TOK // NZ
ROWS = PIECE * GROUP
NG = NZ * NY * NC
TILE_G = 4
NQT = NG // TILE_G
QT = TILE_G * ROWS
KT = 512
SUB = 256
ROUND = 96
BOTH = TOK - ROUND
NKEY = NZ * NX * TOK
NKT = NKEY // KT
CHUNK = NX * TOK
IDS = 72
STEPS = NQT * NKT + 8
SCALE = HD ** -0.5
LOG2E = math.log2(math.e)
BF = jnp.bfloat16
F32 = jnp.float32


def place():
    row = lax.axis_index("row")
    col = lax.axis_index("col")
    z = row // 4
    y = (row // 2) % 2 * 2 + col // 4
    return z, y, col % 4, row % 2


def device(z, y, x, c):
    return (z * 4 + y // 2 * 2 + c, y % 2 * 4 + x)


def origin(z, y, x, c):
    return y // 2 * 2048 + c * 1024 + y % 2 * 512, x * TOK + z * PIECE, c * 2 + y % 2


def tile_start(t, shift):
    return jnp.minimum(t * TILE_G + shift, NG - TILE_G)


class Copies:
    def __init__(self, send, recv):
        self.send, self.recv, self.count, self.all = send, recv, 0, []

    def start(self, src, dst, to):
        i = self.count
        self.count += 1
        copy = pltpu.make_async_remote_copy(
            src_ref=src,
            dst_ref=dst,
            send_sem=self.send.at[i],
            recv_sem=self.recv.at[i],
            device_id=to,
            device_id_type=MESH,
        )
        copy.start()
        self.all.append(copy)
        return copy

    def finish(self):
        for copy in self.all:
            copy.wait_send()


def greet(peers, meanwhile=None):
    barrier = pltpu.get_barrier_semaphore()
    for peer in peers:
        pl.semaphore_signal(barrier, inc=1, device_id=peer, device_id_type=MESH)
    if meanwhile is not None:
        meanwhile()
    pl.semaphore_wait(barrier, len(peers))


N_GATHER = 34 + 9 + 7 + 24 + 4 + 11 + 10


def gather_kernel(
    q_in, k_in, v_in, o_in, do_in, lse_in, seg_in, kv_all, qd_all, keys_t, rows_ref,
    st_all, sg_all, q_ref, o_ref, do_ref, lse_ref, seg_ref, qd_ref, st_ref, send, recv, local,
):
    z, y, x, c = place()
    xp, xm, xo = (x + 1) % NX, (x + 3) % NX, (x + 2) % NX
    yp, ym, yo = (y + 1) % NY, (y + 3) % NY, (y + 2) % NY
    zp, zm = (z + 1) % NZ, (z + NZ - 1) % NZ
    right, left, across = device(z, y, xp, c), device(z, y, xm, c), device(z, y, xo, c)
    up, down, beyond = device(z, yp, x, c), device(z, ym, x, c), device(z, yo, x, c)
    z_right, z_left = device(zp, y, x, c), device(zm, y, x, c)
    twin = device(z, y, x, 1 - c)
    planes = [(z + d) % NZ for d in range(1, NZ)]
    load = [
        pltpu.make_async_copy(src, dst, local.at[i])
        for i, (src, dst) in enumerate([
            (k_in, kv_all.at[z, x, :, pl.ds(0, HD)]),
            (v_in, kv_all.at[z, x, :, pl.ds(HD, HD)]),
            (q_in, q_ref),
            (do_in, do_ref),
            (o_in, o_ref),
            (lse_in, lse_ref),
            (seg_in, seg_ref),
        ])
    ]
    for copy in load:
        copy.start()
    greet(
        [right, left, across, up, down, beyond, twin] + [device(w, y, x, c) for w in planes]
    )
    copies = Copies(send, recv)
    start = copies.start
    yh, yl = y // 2, y % 2

    near, far, hops, pieces, q_near, q_far = {}, {}, {}, {}, {}, []
    few, ends = {}, []
    steps = [0, 1, -1, 2, -2, 3, -3, 4]
    h = TOK // 2

    def block_to(d, to):
        if d != 0:
            src = kv_all.at[(z + NZ + d) % NZ, x]
            return [start(src, src, to)]
        return [
            start(src, kv_all.at[z, x, :, pl.ds(i * HD, HD)], to)
            for i, src in enumerate((k_in, v_in))
        ]

    def ring(s):
        if 0 < s < 4:
            for copy in hops["r", s]:
                copy.wait_recv()
        if s < 3:
            hops["r", s + 1] = block_to(-s, z_right)
        if s > 0:
            for copy in hops["l", s]:
                copy.wait_recv()
        if s < 4:
            hops["l", s + 1] = block_to(s, z_left)

    def spread(d):
        near[d] = (block_to(d, right), block_to(d, left))

    def pass_on(d):
        zb = (z + NZ + d) % NZ
        for copy in near[d][0]:
            copy.wait_recv()
        src = kv_all.at[zb, xm, pl.ds(0, h)]
        far[d] = [start(src, src, right)]
        for copy in near[d][1]:
            copy.wait_recv()
        src = kv_all.at[zb, xp, pl.ds(h, h)]
        far[d].append(start(src, src, left))

    def pack(_):
        load[2].wait()
        load[3].wait()
        for w in range(NZ):
            for g in range(GROUP):
                here = (slice(w * PIECE, (w + 1) * PIECE), slice(g * HD, (g + 1) * HD))
                there = slice(g * PIECE, (g + 1) * PIECE)
                qd_ref[w, 0, there] = q_ref[here]
                qd_ref[w, 1, there] = do_ref[here]
        qd_all[z, yh, c, yl] = qd_ref[z]

    def q_send(d):
        w = (z + NZ + d) % NZ
        pieces[d] = start(qd_ref.at[w], qd_all.at[z, yh, c, yl], device(w, y, x, c))

    def q_share(d):
        if d != 0:
            pieces[d].wait_recv()
        src = qd_all.at[(z + NZ - d) % NZ, yh, c, yl]
        q_near[d] = (start(src, src, up), start(src, src, down))

    def q_pass(d):
        zz = (z + NZ - d) % NZ
        q_near[d][0].wait_recv()
        q_near[d][1].wait_recv()
        if steps.index(d) % 2 == 0:
            src = qd_all.at[zz, ym // 2, c, ym % 2]
            q_far.append(start(src, src, up))
        else:
            src = qd_all.at[zz, yp // 2, c, yp % 2]
            q_far.append(start(src, src, down))

    def q_across(where):
        if where == 2:
            for copy in q_far:
                copy.wait_recv()
        for yy in ((y,), (yp, ym), (yo,))[where]:
            src = qd_all.at[:, yy // 2, c, yy % 2]
            ends.append(start(src, src, twin))

    def stats(stage):
        if stage == 0:
            for copy in load[4:]:
                copy.wait()
            sub = lax.broadcasted_iota(jnp.int32, (TOK, TOK), 0)
            lane = lax.broadcasted_iota(jnp.int32, (TOK, TOK), 1)
            dots = []
            for g in range(GROUP):
                cols = slice(g * HD, (g + 1) * HD)
                both = lax.dot_general(
                    do_ref[:, cols], o_ref[:, cols], (((1,), (1,)), ((), ())),
                    preferred_element_type=F32,
                )
                dots.append(jnp.sum(jnp.where(sub == lane, both, 0.0), axis=0, keepdims=True))
            numbers = jnp.concatenate([lse_ref[...]] + dots, axis=0)
            seg = seg_ref[...].astype(F32)
            sg_all[z, x] = seg
            segs = jnp.broadcast_to(seg, (2 * GROUP, TOK))
            sub, block = sub[0:8], lane[0:8] // PIECE
            turned = [
                [a if d == 0 else pltpu.roll(a, d * PIECE, 1) for d in range(NZ)]
                for a in (numbers, segs)
            ]
            for w in range(NZ):
                for i in range(2):
                    row = jnp.zeros((8, TOK), F32)
                    for d in range(NZ):
                        fits = (block == sub) & ((sub + NZ - w) % NZ == d)
                        row += jnp.where(fits, turned[i][d], 0.0)
                    st_ref[w, i:i + 1, :] = jnp.sum(row, axis=0, keepdims=True)
            st_all[z, yh, c, yl] = st_ref[z]
            few[0] = [
                start(st_ref.at[w], st_all.at[z, yh, c, yl], device(w, y, x, c)) for w in planes
            ]
            src = sg_all.at[z, x]
            few[0] += [start(src, src, device(w, y, x, c)) for w in planes]
        elif stage == 1:
            for copy in few[0]:
                copy.wait_recv()
            src = st_all.at[:, yh, c, yl]
            few[1] = [start(src, src, to) for to in (up, down, beyond)]
            src = sg_all.at[:, x]
            few[2] = [start(src, src, to) for to in (right, left, across)]
        else:
            for copy in few[1]:
                copy.wait_recv()
            src = st_all.at[:, :, c]
            few[2].append(start(src, src, twin))

    def turn(d):
        zb = (z + NZ + d) % NZ
        for copy in far[d]:
            copy.wait_recv()
        if d == 0:
            load[0].wait()
            load[1].wait()
        for i in range(NX):
            keys_t[zb, :, i * TOK:(i + 1) * TOK] = kv_all[zb, i, :, 0:HD].T

    def ranges(_):
        for copy in few[2]:
            copy.wait_recv()
        key_start, query_start, shift = origin(z, y, x, c)
        ids = lax.broadcasted_iota(jnp.int32, (IDS, TOK), 0).astype(F32)
        before = jnp.zeros((IDS, TOK), F32)
        for zz in range(NZ):
            for xx in range(NX):
                before += jnp.where(sg_all[zz, xx] < ids, 1.0, 0.0)
        before = jnp.sum(before, axis=1, keepdims=True)
        id_col = lax.broadcasted_iota(jnp.int32, (IDS, QT), 0).astype(F32)
        half = lax.broadcasted_iota(jnp.int32, (1, 128), 1) < ROWS
        lane = lax.broadcasted_iota(jnp.int32, (1, QT), 1)

        def one_tile(t, carry):
            first = t * TILE_G + shift
            g = tile_start(t, shift)

            def numbers(i, row):
                p = g + i
                return st_all[p // 8, p // 4 % 2, p // 2 % 2, p % 2, row:row + 1, :]

            def pair(a, b):
                return jnp.where(half, a, b)

            own = [numbers(i, 0) for i in range(TILE_G)]
            over = [pltpu.roll(a, ROWS, 1) for a in own]
            lse = jnp.concatenate([pair(own[0], over[1]), pair(own[2], over[3])], axis=1)
            dot = jnp.concatenate([pair(over[0], own[1]), pair(over[2], own[3])], axis=1)
            seg = [numbers(i, 1) for i in range(TILE_G)]
            seg = jnp.concatenate([pair(seg[0], seg[1]), pair(seg[2], seg[3])], axis=1)
            lo = jnp.sum(jnp.where(id_col == seg, before, 0.0), axis=0, keepdims=True)
            piece = g + lane // ROWS
            rem = piece % NZ * CHUNK + query_start + lane % PIECE - key_start
            hi = piece // NZ * CHUNK + jnp.clip(rem + 1, 0, CHUNK)
            fresh = piece >= first
            rows_ref[t, 0:1, :] = lse * LOG2E
            rows_ref[t, 1:2, :] = dot
            rows_ref[t, 2:3, :] = jnp.where(fresh, lo, float(NKEY))
            rows_ref[t, 3:4, :] = jnp.where(fresh, hi, 0).astype(F32)
            return carry

        lax.fori_loop(0, NQT, one_tile, 0)

    for do, which in [
        (spread, 0), (ring, 0), (pack, 0), (q_send, -1), (q_share, 0), (q_send, 3), (q_send, -2),
        (ring, 1), (q_send, -3), (q_send, 1), (spread, 1), (q_send, 4), (pass_on, 0),
        (spread, -1), (stats, 0), (q_share, 3), (q_share, -1), (ring, 2), (spread, -2),
        (q_send, 2), (spread, 2), (q_pass, 3), (pass_on, -1), (q_share, -2), (stats, 1),
        (q_pass, 0), (pass_on, -2), (q_share, 4), (pass_on, 1), (ring, 3), (q_share, 1),
        (spread, -3), (q_share, -3), (spread, 3), (q_share, 2), (q_pass, -2), (stats, 2),
        (turn, -2), (turn, -1), (q_pass, 1), (q_pass, 4), (q_across, 0), (q_pass, -1), (ring, 4),
        (spread, 4), (pass_on, 2), (pass_on, -3), (q_pass, -3), (q_pass, 2), (q_across, 1),
        (ranges, 0), (turn, 1), (pass_on, 3), (pass_on, 4), (q_across, 2), (turn, 2), (turn, 0),
        (turn, 3), (turn, -3), (turn, 4),
    ]:
        do(which)
    for copy in ends:
        copy.wait_recv()
    assert copies.count == N_GATHER, copies.count
    copies.finish()


def attend_kernel(
    kv_ref, qd_ref, keys_t, rows_ref, dq_acc, dk_acc, dv_acc, p_ref, ds_ref,
    low_ref, k_list, t_list, from_list,
):
    z, y, x, c = place()
    shift = origin(z, y, x, c)[2]

    def piece(t):
        return tile_start(t, shift)

    for t in range(NQT):
        low_ref[t] = jnp.min(rows_ref[t, 2:3, :]).astype(jnp.int32)

    def clear(k, carry):
        dq_acc[2 * k] = jnp.zeros((HD, QT), F32)
        dq_acc[2 * k + 1] = jnp.zeros((HD, QT), F32)
        dk_acc[k] = jnp.zeros((KT, HD), F32)
        dv_acc[k] = jnp.zeros((KT, HD), F32)
        return carry

    lax.fori_loop(0, NKT, clear, 0)

    def nothing(n):
        k_list[n] = 0
        t_list[n] = 0
        from_list[n] = -(1 << 20)

    lows = [low_ref[t] for t in range(NQT)]

    def listed(k, count):
        end = 0
        for low in lows:
            end += jnp.where(low < (k + 1) * KT, 1, 0)

        def note(t, count):
            k_list[count] = k
            t_list[count] = t
            from_list[count] = k * KT
            return count + 1

        return lax.fori_loop(2 * k + y // 2, end, note, count)

    count = lax.fori_loop(0, NKT, listed, 0)
    nothing(count)

    def sums(n, slot):
        k, t = k_list[n], t_list[n]
        q = qd_ref[pl.ds(piece(t), TILE_G), 0].reshape(QT, HD)
        do = qd_ref[pl.ds(piece(t), TILE_G), 1].reshape(QT, HD)
        p, ds = p_ref[slot], ds_ref[slot]
        dv_acc[k] += jnp.dot(p, do, preferred_element_type=F32)
        dk_acc[k] += jnp.dot(ds, q, preferred_element_type=F32)
        dq_acc[t] += jnp.dot(keys_t[k], ds, preferred_element_type=F32)

    def probabilities(n, slot):
        k, t = k_list[n], t_list[n]
        q = qd_ref[pl.ds(piece(t), TILE_G), 0].reshape(QT, HD)
        do = qd_ref[pl.ds(piece(t), TILE_G), 1].reshape(QT, HD)
        start = from_list[n].astype(F32)
        low = rows_ref[t, 2:3, :] - start
        high = rows_ref[t, 3:4, :] - start
        across = (((1,), (1,)), ((), ()))
        for i in range(KT // SUB):
            part = pl.ds(i * SUB, SUB)
            s = lax.dot_general(kv_ref[k, part, 0:HD], q, across, preferred_element_type=F32)
            dp = lax.dot_general(
                kv_ref[k, part, HD:2 * HD], do, across, preferred_element_type=F32
            )
            index = (lax.broadcasted_iota(jnp.int32, (SUB, QT), 0) + i * SUB).astype(F32)
            p = jnp.exp2(s * (SCALE * LOG2E) - rows_ref[t, 0:1, :])
            p = jnp.where((index >= low) & (index < high), p, 0.0)
            p_ref[slot, part, :] = p.astype(BF)
            ds_ref[slot, part, :] = (p * (dp - rows_ref[t, 1:2, :])).astype(BF)

    def step(i, carry):
        n = 2 * i
        sums(n, 0)
        sums(n + 1, 1)
        probabilities(n + 2, 0)
        probabilities(n + 3, 1)
        return carry

    steps = (count + 1) // 2
    probabilities(0, 0)
    probabilities(1, 1)
    lax.fori_loop(0, steps - 1, step, 0)
    sums(2 * steps - 2, 0)
    sums(2 * steps - 1, 1)


N_REDUCE = 16 + 16 + 7 + 7 + 4 + 1 + 2 + 2 + 7


def reduce_kernel(
    dq_acc, dk_acc, dv_acc, gq_ref, gkv_ref, kv_ref, dq_in,
    far, near, out_x, ring_in, ring_out, both_in, both_out, both_sum, b_far, b_near, b_out,
    q_twin, q_sum, q_far, q_near, q_out, q_send, q_back, send, recv,
):
    z, y, x, c = place()
    xp, xm, xo = (x + 1) % NX, (x + 3) % NX, (x + 2) % NX
    yp, ym, yo = (y + 1) % NY, (y + 3) % NY, (y + 2) % NY
    zp, zm = (z + 1) % NZ, (z + NZ - 1) % NZ
    right, left = device(z, y, xp, c), device(z, y, xm, c)
    up, down = device(z, yp, x, c), device(z, ym, x, c)
    z_right, z_left = device(zp, y, x, c), device(zm, y, x, c)
    twin = device(z, y, x, 1 - c)
    planes = [(z + d) % NZ for d in range(1, NZ)]
    shift = origin(z, y, x, c)[2]

    def rounded():
        def keys_side(k, carry):
            for i in range(NX):
                part = pl.ds(i * TOK, TOK)
                kv_ref[k, i, :, 0:HD] = (dk_acc[k, part] * SCALE).astype(BF)
                kv_ref[k, i, :, HD:2 * HD] = dv_acc[k, part].astype(BF)
            return carry

        def queries_side(i, carry):
            for j in range(2):
                t = NQT - 1 - 2 * i - j
                dq = (dq_acc[t] * SCALE).astype(BF).T.reshape(TILE_G, ROWS, HD)
                for e in range(TILE_G):
                    g = tile_start(t, shift) + e
                    dq_in[g // 8, g // 4 % 2, g // 2 % 2, g % 2] = dq[e]
            return carry

        for g in range(TILE_G):
            dq_in[0, 0, g // 2, g % 2] = jnp.zeros((ROWS, HD), BF)
        lax.fori_loop(0, NQT // 2, queries_side, 0)
        lax.fori_loop(0, NKT, keys_side, 0)

    greet([right, left, up, down, twin] + [device(w, y, x, c) for w in planes], rounded)
    copies = Copies(send, recv)
    start = copies.start
    h = ROUND // 2
    rest = pl.ds(ROUND, BOTH)
    order = [4, 3, -3, 2, -2, 1, -1, 0]

    def first(n):
        zb = (z + NZ + order[n]) % NZ
        return (
            start(kv_ref.at[zb, xo, pl.ds(0, h)], far.at[n, 0], right),
            start(kv_ref.at[zb, xo, pl.ds(h, h)], far.at[n, 1], left),
        )

    def second(n, pair):
        zb = (z + NZ + order[n]) % NZ
        pair[0].wait_recv()
        out_x[n, 0, 0:h] = (kv_ref[zb, xp, 0:h].astype(F32) + far[n, 0].astype(F32)).astype(BF)
        out_x[n, 0, h:ROUND] = kv_ref[zb, xp, h:ROUND]
        a = start(out_x.at[n, 0], near.at[n, 0], right)
        pair[1].wait_recv()
        out_x[n, 1, 0:h] = kv_ref[zb, xm, 0:h]
        out_x[n, 1, h:ROUND] = (kv_ref[zb, xm, h:ROUND].astype(F32) + far[n, 1].astype(F32)).astype(BF)
        b = start(out_x.at[n, 1], near.at[n, 1], left)
        return a, b

    ring = {}

    def third(n, pair):
        off = order[n]
        zb = (z + NZ + off) % NZ
        pair[0].wait_recv()
        pair[1].wait_recv()
        total = kv_ref[zb, x, 0:ROUND].astype(F32) + near[n, 0].astype(F32) + near[n, 1].astype(F32)
        if off > 0:
            hop = 4 - off
            if hop > 0:
                ring[("r", hop)].wait_recv()
                total += ring_in[hop - 1].astype(F32)
            ring_out[n] = total.astype(BF)
            ring[("r", hop + 1)] = start(ring_out.at[n], ring_in.at[hop], z_right)
        elif off < 0:
            hop = 3 + off
            if hop > 0:
                ring[("l", hop)].wait_recv()
                total += ring_in[4 + hop - 1].astype(F32)
            ring_out[n] = total.astype(BF)
            ring[("l", hop + 1)] = start(ring_out.at[n], ring_in.at[4 + hop], z_left)
        else:
            ring[("r", 4)].wait_recv()
            ring[("l", 3)].wait_recv()
            total += ring_in[3].astype(F32) + ring_in[6].astype(F32)
            gkv_ref[0:ROUND] = total.astype(BF)

    def both(s):
        if s == 0:
            ring["R", 1] = start(kv_ref.at[(z + 3) % NZ, :, rest], both_in.at[0], z_right)
            ring["L", 1] = start(kv_ref.at[(z + 4) % NZ, :, rest], both_in.at[3], z_left)
            return
        if s < 4:
            ring["R", s].wait_recv()
        if s < 3:
            mine = kv_ref[(z + 3 - s) % NZ, :, ROUND:TOK].astype(F32)
            both_out[s - 1] = (mine + both_in[s - 1].astype(F32)).astype(BF)
            ring["R", s + 1] = start(both_out.at[s - 1], both_in.at[s], z_right)
        if s < 5:
            ring["L", s].wait_recv()
        if s < 4:
            mine = kv_ref[(z + 4 + s) % NZ, :, ROUND:TOK].astype(F32)
            both_out[1 + s] = (mine + both_in[2 + s].astype(F32)).astype(BF)
            ring["L", s + 1] = start(both_out.at[1 + s], both_in.at[3 + s], z_left)
        if s == 4:
            both_sum[...] = (
                kv_ref[z, :, ROUND:TOK].astype(F32)
                + both_in[2].astype(F32)
                + both_in[6].astype(F32)
            ).astype(BF)
            b = BOTH // 2
            ring["f", 0] = start(both_sum.at[xo, pl.ds(0, b)], b_far.at[0], right)
            ring["f", 1] = start(both_sum.at[xo, pl.ds(b, b)], b_far.at[1], left)
        if s == 5:
            b = BOTH // 2
            ring["f", 0].wait_recv()
            b_out[0, 0:b] = (both_sum[xp, 0:b].astype(F32) + b_far[0].astype(F32)).astype(BF)
            b_out[0, b:BOTH] = both_sum[xp, b:BOTH]
            ring["n", 0] = start(b_out.at[0], b_near.at[0], right)
            ring["f", 1].wait_recv()
            b_out[1, 0:b] = both_sum[xm, 0:b]
            b_out[1, b:BOTH] = (both_sum[xm, b:BOTH].astype(F32) + b_far[1].astype(F32)).astype(BF)
            ring["n", 1] = start(b_out.at[1], b_near.at[1], left)

    def both_end():
        ring["n", 0].wait_recv()
        ring["n", 1].wait_recv()
        total = both_sum[x].astype(F32) + b_near[0].astype(F32) + b_near[1].astype(F32)
        gkv_ref[ROUND:TOK] = total.astype(BF)

    queue = {}

    def q_step(s):
        if s == 0:
            queue["twin"] = start(dq_in.at[:, :, 1 - c], q_twin, twin)
        elif s == 1:
            queue["twin"].wait_recv()
            for zz in range(NZ):
                q_sum[zz] = (dq_in[zz, :, c].astype(F32) + q_twin[zz].astype(F32)).astype(BF)
            queue["a"] = start(q_sum.at[pl.ds(0, 4), yo // 2, yo % 2], q_far.at[0], up)
            queue["b"] = start(q_sum.at[pl.ds(4, 4), yo // 2, yo % 2], q_far.at[1], down)
        elif s == 2:
            queue["a"].wait_recv()
            q_out[0, 0:4] = (
                q_sum[0:4, yp // 2, yp % 2].astype(F32) + q_far[0].astype(F32)
            ).astype(BF)
            q_out[0, 4:8] = q_sum[4:8, yp // 2, yp % 2]
            queue["c"] = start(q_out.at[0], q_near.at[0], up)
            queue["b"].wait_recv()
            q_out[1, 0:4] = q_sum[0:4, ym // 2, ym % 2]
            q_out[1, 4:8] = (
                q_sum[4:8, ym // 2, ym % 2].astype(F32) + q_far[1].astype(F32)
            ).astype(BF)
            queue["d"] = start(q_out.at[1], q_near.at[1], down)
        else:
            queue["c"].wait_recv()
            queue["d"].wait_recv()
            q_send[...] = (
                q_sum[:, y // 2, y % 2].astype(F32)
                + q_near[0].astype(F32)
                + q_near[1].astype(F32)
            ).astype(BF)
            queue["back"] = [
                start(q_send.at[w], q_back.at[z], device(w, y, x, c)) for w in planes
            ]
            q_back[z] = q_send[z]

    one, two = {}, {}

    def x_far(n):
        one[n] = first(n)

    def x_near(n):
        two[n] = second(n, one[n])

    def x_sum(n):
        third(n, two[n])

    for do, which in [
        (q_step, 0), (x_far, 0), (both, 0), (x_far, 1), (x_far, 2), (x_far, 3), (x_near, 0),
        (x_far, 4), (x_far, 5), (both, 1), (q_step, 1), (x_near, 1), (x_near, 2), (x_sum, 0),
        (x_far, 6), (x_near, 3), (x_near, 4), (x_far, 7), (both, 2), (q_step, 2), (x_near, 5),
        (x_sum, 1), (x_sum, 2), (x_near, 6), (both, 3), (x_sum, 3), (x_sum, 4), (q_step, 3),
        (both, 4), (x_sum, 5), (x_near, 7), (x_sum, 6), (both, 5), (x_sum, 7),
    ]:
        do(which)
    both_end()
    for copy in queue["back"]:
        copy.wait_recv()
    for w in range(NZ):
        for g in range(GROUP):
            rows = slice(w * PIECE, (w + 1) * PIECE)
            gq_ref[rows, g * HD:(g + 1) * HD] = q_back[w, g * PIECE:(g + 1) * PIECE]
    assert copies.count == N_REDUCE, copies.count
    copies.finish()


def body(queries, keys, values, outputs, out_grad, log_sum_exp, segment_ids):
    hbm = pl.BlockSpec(memory_space=pltpu.HBM)
    vmem = pl.BlockSpec(memory_space=pltpu.VMEM)

    kv_all, qd_all, keys_t, row_data = pl.pallas_call(
        gather_kernel,
        out_shape=[
            jax.ShapeDtypeStruct((NZ, NX, TOK, 2 * HD), BF),
            jax.ShapeDtypeStruct((NZ, 2, NC, 2, 2, ROWS, HD), BF),
            jax.ShapeDtypeStruct((NKT, HD, KT), BF),
            jax.ShapeDtypeStruct((NQT, 8, QT), F32),
        ],
        in_specs=[hbm] * 7,
        out_specs=[vmem] * 4,
        scratch_shapes=[
            pltpu.VMEM((NZ, 2, NC, 2, 2, 128), F32),
            pltpu.VMEM((NZ, NX, 1, TOK), F32),
            pltpu.VMEM((TOK, GROUP * HD), BF),
            pltpu.VMEM((TOK, GROUP * HD), BF),
            pltpu.VMEM((TOK, GROUP * HD), BF),
            pltpu.VMEM((GROUP, TOK), F32),
            pltpu.VMEM((1, TOK), jnp.int32),
            pltpu.VMEM((NZ, 2, ROWS, HD), BF),
            pltpu.VMEM((NZ, 2, 2 * ROWS), F32),
            pltpu.SemaphoreType.DMA((N_GATHER,)),
            pltpu.SemaphoreType.DMA((N_GATHER,)),
            pltpu.SemaphoreType.DMA((7,)),
        ],
        compiler_params=pltpu.CompilerParams(
            collective_id=0, has_side_effects=True, vmem_limit_bytes=40 * 2**20
        ),
        name="gather",
    )(
        *[
            pltpu.with_memory_space_constraint(a, pltpu.HBM)
            for a in (
                queries, keys, values, outputs, out_grad,
                log_sum_exp.T, segment_ids.reshape(1, TOK),
            )
        ]
    )

    sums = pl.pallas_call(
        attend_kernel,
        out_shape=[
            jax.ShapeDtypeStruct((NQT, HD, QT), F32),
            jax.ShapeDtypeStruct((NKT, KT, HD), F32),
            jax.ShapeDtypeStruct((NKT, KT, HD), F32),
        ],
        in_specs=[vmem] * 4,
        out_specs=[vmem] * 3,
        scratch_shapes=[
            pltpu.VMEM((2, KT, QT), BF),
            pltpu.VMEM((2, KT, QT), BF),
            pltpu.SMEM((NQT,), jnp.int32),
            pltpu.SMEM((STEPS,), jnp.int32),
            pltpu.SMEM((STEPS,), jnp.int32),
            pltpu.SMEM((STEPS,), jnp.int32),
        ],
        compiler_params=pltpu.CompilerParams(vmem_limit_bytes=40 * 2**20),
        name="attend",
    )(
        kv_all.reshape(NKT, KT, 2 * HD),
        qd_all.reshape(NG, 2, ROWS, HD),
        keys_t,
        row_data,
    )

    grad_q, grad_kv = pl.pallas_call(
        reduce_kernel,
        out_shape=[
            jax.ShapeDtypeStruct((TOK, GROUP * HD), BF),
            jax.ShapeDtypeStruct((TOK, 2 * HD), BF),
        ],
        in_specs=[vmem] * 3,
        out_specs=[vmem] * 2,
        scratch_shapes=[
            pltpu.VMEM((NZ, NX, TOK, 2 * HD), BF),
            pltpu.VMEM((NZ, 2, NC, 2, ROWS, HD), BF),
            pltpu.VMEM((NZ, 2, ROUND // 2, 2 * HD), BF),
            pltpu.VMEM((NZ, 2, ROUND, 2 * HD), BF),
            pltpu.VMEM((NZ, 2, ROUND, 2 * HD), BF),
            pltpu.VMEM((7, ROUND, 2 * HD), BF),
            pltpu.VMEM((7, ROUND, 2 * HD), BF),
            pltpu.VMEM((7, NX, BOTH, 2 * HD), BF),
            pltpu.VMEM((5, NX, BOTH, 2 * HD), BF),
            pltpu.VMEM((NX, BOTH, 2 * HD), BF),
            pltpu.VMEM((2, BOTH // 2, 2 * HD), BF),
            pltpu.VMEM((2, BOTH, 2 * HD), BF),
            pltpu.VMEM((2, BOTH, 2 * HD), BF),
            pltpu.VMEM((NZ, 2, 2, ROWS, HD), BF),
            pltpu.VMEM((NZ, 2, 2, ROWS, HD), BF),
            pltpu.VMEM((2, 4, ROWS, HD), BF),
            pltpu.VMEM((2, NZ, ROWS, HD), BF),
            pltpu.VMEM((2, NZ, ROWS, HD), BF),
            pltpu.VMEM((NZ, ROWS, HD), BF),
            pltpu.VMEM((NZ, ROWS, HD), BF),
            pltpu.SemaphoreType.DMA((N_REDUCE,)),
            pltpu.SemaphoreType.DMA((N_REDUCE,)),
        ],
        compiler_params=pltpu.CompilerParams(
            collective_id=1, has_side_effects=True, vmem_limit_bytes=40 * 2**20
        ),
        name="reduce",
    )(*sums)
    return grad_q, grad_kv[:, :HD], grad_kv[:, HD:]


def solution(mesh):
    rows = P(("row", "col"), None)
    return jax.shard_map(
        body,
        mesh=mesh,
        in_specs=(rows, rows, rows, rows, rows, rows, P(("row", "col"))),
        out_specs=(rows, rows, rows),
        check_vma=False,
    )
```
